512 devices in a mesh: section: 64 (over y, z_lo, core), expert: 8 (over x, z_hi).
Axes of the slice: x: 4, y: 4, z: 16 (z_hi: 2, z_lo: 8; z = z_hi * 8 + z_lo), core: 2. Of those that a mesh axis runs over, the one named last changes fastest.
Arguments:
- up_in: bfloat16 [64, 512, 3584], P('section', 'expert'), may hold values from -6 to 6
- down_in: bfloat16 [64, 512, 3584], P('section', 'expert'), may hold values from -6 to 6
- router: float32 [64, 3584], P('section'), may hold values from -0.1875 to 0.1875
- w_gate: bfloat16 [64, 3584, 1024], P('section', None, 'expert'), may hold values from -0.09375 to 0.09375
- w_up: bfloat16 [64, 3584, 1024], P('section', None, 'expert'), may hold values from -0.09375 to 0.09375
- w_down: bfloat16 [64, 1024, 3584], P('section', 'expert'), may hold values from -0.375 to 0.375
- slots_up: int32 [64, 2, 8, 64], P('section', None, 'expert'), may hold values from 0 to 63, each once within a row
- slots_down: int32 [64, 2, 8, 64], P('section', None, 'expert'), may hold values from 0 to 63, each once within a row
Outputs:
- up_out: bfloat16 [64, 512, 3584], P('section', 'expert')
- down_out: bfloat16 [64, 512, 3584], P('section', 'expert')
The draws below stay inside these ranges and needn't reach their ends.
Inputs may be any that keep to these rules, and one draw needn't show every extreme that they name: `slots_up`: each device's 64 tokens of a micro-batch at a step hold the slots 0 to 63 once each. `slots_down`: each device's 64 tokens of a micro-batch at a step hold the slots 0 to 63 once each.
All inputs are finite; a program needn't handle non-finite values.
Results may differ from the reference program's by a relative error of at most 0.01.
Values may be sent and summed in bfloat16 or wider, within the bound.
A program may use at most 64 MiB of HBM per device.

```python
import jax
import jax.numpy as jnp
from jax import lax

D = 3584
FF = 1024
MB_DEV = 64
CAP = 18
TICKS = 2
TOK_ST = 512
N_SECTION = 64
N_EXPERT = 8


def block_scale(key, dims, shards, least, high):
    loudness = 1.0
    for position, shards_of in shards:
        draws = jax.random.uniform(jax.random.fold_in(jax.random.fold_in(key, 6), position), (shards_of,), jnp.float32, least / len(shards), high / len(shards))
        loudness = loudness * jnp.repeat(jnp.exp(draws), dims[position] // shards_of).reshape((-1,) + (1,) * (len(dims) - 1 - position))
    return loudness


def bell_draw(key, extent, deviation, reach, pieces=(), kind=jnp.bfloat16):
    factor_of = block_scale(key, extent, pieces, -0.22, 0.18) if pieces else 1.0
    values = jax.random.normal(key, extent, jnp.float32) * deviation * factor_of
    return jnp.minimum(jnp.maximum(values, -reach), reach).astype(kind)


def setup_inputs(seed: int = 0) -> dict:
    splits = jax.random.split(jax.random.key(seed), 9)
    return {
        "up_in": bell_draw(splits[0], (N_SECTION, TOK_ST, D), 1.0, 6.0, ((0, 64), (1, 8))),
        "down_in": bell_draw(splits[1], (N_SECTION, TOK_ST, D), 1.0, 6.0, ((0, 64), (1, 8))),
        "router": bell_draw(splits[2], (N_SECTION, D), (D // 4) ** -0.5, 0.1875, ((0, 64),), jnp.float32),
        "w_gate": bell_draw(splits[3], (N_SECTION, D, FF), D ** -0.5, 0.09375, ((0, 64), (2, 8))),
        "w_up": bell_draw(splits[4], (N_SECTION, D, FF), D ** -0.5, 0.09375, ((0, 64), (2, 8))),
        "w_down": bell_draw(splits[5], (N_SECTION, FF, D), (FF // 4) ** -0.5, 0.375, ((0, 64), (1, 8))),
        "slots_up": jax.vmap(lambda own: jax.random.permutation(own, MB_DEV))(jax.random.split(splits[6], N_SECTION * TICKS * N_EXPERT)).reshape((N_SECTION, TICKS, N_EXPERT, MB_DEV)).astype(jnp.int32),
        "slots_down": jax.vmap(lambda own: jax.random.permutation(own, MB_DEV))(jax.random.split(splits[7], N_SECTION * TICKS * N_EXPERT)).reshape((N_SECTION, TICKS, N_EXPERT, MB_DEV)).astype(jnp.int32),
    }


def layer(x, slots, router, w_gate, w_up, w_down):
    xf = x.astype(jnp.float32).reshape(N_EXPERT, MB_DEV, D)
    normed = xf * lax.rsqrt(lax.optimization_barrier(jnp.mean(xf * xf, axis=-1, keepdims=True)) + 1e-06)
    affinity = jax.nn.sigmoid(jnp.dot(normed, router, precision=lax.Precision.HIGHEST))
    normed_low = normed.astype(jnp.bfloat16)

    def place(rows, slot_row):
        return jnp.zeros((CAP, D), jnp.bfloat16).at[slot_row].set(rows, mode='drop')
    blocks = jax.vmap(place)(normed_low, slots).reshape(N_EXPERT * CAP, D)
    gate = jnp.dot(blocks, w_gate, preferred_element_type=jnp.float32)
    upper = jnp.dot(blocks, w_up, preferred_element_type=jnp.float32)
    hidden = (jax.nn.silu(gate) * upper).astype(jnp.bfloat16)
    hidden_groups = hidden.reshape(N_EXPERT * CAP, N_EXPERT, FF // N_EXPERT).astype(jnp.float32)
    down_groups = w_down.reshape(N_EXPERT, FF // N_EXPERT, D).astype(jnp.float32)
    partial_sums = jnp.einsum('rgf,gfd->grd', hidden_groups, down_groups)
    rounded = lax.optimization_barrier(partial_sums.astype(jnp.bfloat16))
    expert_out = lax.optimization_barrier(jnp.sum(rounded.astype(jnp.float32), axis=0)).reshape(N_EXPERT, CAP, D)

    def take(out_rows, slot_row):
        picked = out_rows[jnp.minimum(slot_row, CAP - 1)]
        return jnp.where((slot_row < CAP)[:, None], picked, jnp.float32(0.0))
    taken = jax.vmap(take)(expert_out, slots)
    result = xf + affinity[..., None] * taken
    return result.astype(jnp.bfloat16).reshape(N_EXPERT * MB_DEV, D)

def all_sections(acts, slots, step, router, w_gate, w_up, w_down):

    def one_section(items):
        return layer(items[0], items[1][step], items[2], items[3], items[4], items[5])
    return lax.map(one_section, (acts, slots, router, w_gate, w_up, w_down))

def reference(up_in, down_in, router, w_gate, w_up, w_down, slots_up, slots_down):
    mid_up = all_sections(up_in, slots_up, 0, router, w_gate, w_up, w_down)
    mid_down = all_sections(down_in, slots_down, 0, router, w_gate, w_up, w_down)
    empty = jnp.zeros_like(mid_up[:1])
    moved_up = jnp.concatenate([empty, mid_up[:-1]], axis=0)
    moved_down = jnp.concatenate([mid_down[1:], empty], axis=0)
    up_out = all_sections(moved_up, slots_up, 1, router, w_gate, w_up, w_down)
    down_out = all_sections(moved_down, slots_down, 1, router, w_gate, w_up, w_down)
    return (up_out, down_out)
```

```python
import functools

import jax
import jax.numpy as jnp
from jax import lax
from jax.experimental import pallas as pl
from jax.experimental.pallas import tpu as pltpu
from jax.sharding import PartitionSpec as P

MESH = pl.DeviceIdType.MESH
CAP = 18
MAIN = 16
G = 512
EPS = 1e-06
F32 = jnp.float32
BF16 = jnp.bfloat16


def iota(shape, axis):
    return lax.broadcasted_iota(jnp.int32, shape, axis)


def slot_of_row(row, k):
    tail = row - MAIN - 2 * k
    return jnp.where(
        row < MAIN, row, jnp.where((tail >= 0) & (tail < CAP - MAIN), MAIN + tail, -1)
    )


def dot(a, b):
    return jnp.dot(a, b, preferred_element_type=F32)


def kernel(
    up_ref, dn_ref, router_ref, su_ref, sd_ref, wg_hbm, wu_hbm, wd_hbm,
    uo_ref, do_ref,
    g_ref, p_ref, r0_ref, r1_ref, zs_ref, zr_ref, b2_ref, m1_ref, m2_ref, aff_ref,
    mys_ref, nbs_ref, wgu_ref, wd_ref, chunks, sections,
    w_sem, agz_s, agz_r, agx_s, agx_r, ago_s, ago_r, own_s, own_r,
    rs1_s, rs1_r, rs0_s, rs0_r, rsz_s, rsz_r, m_s, m_r, n_s, n_r,
):
    s = lax.axis_index("section")
    e = lax.axis_index("expert")
    x = e // 2
    h = e % 2
    other = x * 2 + (1 - h)
    width = up_ref.shape[2]
    groups = width // G
    tokens = up_ref.shape[1]
    in_refs = (up_ref, dn_ref)
    out_refs = (uo_ref, do_ref)
    slot_refs = (su_ref, sd_ref)
    cols = [pl.ds(a * G, (b - a) * G) for a, b in chunks]

    def peer(d):
        return lax.rem(x + d, 4)

    def xdev(d):
        return (s, peer(d) * 2 + h)

    zdev = (s, other)
    step_of = (1, -1)
    has_next = (s < sections - 1, s > 0)
    has_prev = (s > 0, s < sections - 1)

    def remote(src, dst, ssem, rsem, device):
        return pltpu.make_async_remote_copy(
            src_ref=src, dst_ref=dst, send_sem=ssem, recv_sem=rsem,
            device_id=device, device_id_type=MESH,
        )

    def agz(p, st, c):
        if p == 0:
            src, device = g_ref.at[p, st, x, :, cols[c]], zdev
        else:
            src, device = b2_ref.at[st, :, cols[c]], (s + step_of[st], other)
        return remote(
            src, g_ref.at[p, st, 4 + x, :, cols[c]],
            agz_s.at[p, st, c], agz_r.at[p, st, c], device,
        )

    def agx(p, st, d, c):
        blk = g_ref.at[p, st, 4 + x, :, cols[c]]
        return remote(blk, blk, agx_s.at[p, st, d - 1, c], agx_r.at[p, st, d - 1, c], xdev(d))

    def ago(p, st, d):
        blk = g_ref.at[p, st, x]
        return remote(blk, blk, ago_s.at[p, st, d - 1], ago_r.at[p, st, d - 1], xdev(d))

    def own(st):
        return remote(
            b2_ref.at[st], g_ref.at[1, st, x], own_s.at[st], own_r.at[st],
            (s + step_of[st], e),
        )

    def rs1(p, st, d, c):
        return remote(
            p_ref.at[p, st, 4 + peer(d), :, cols[c]], r1_ref.at[p, st, d - 1, :, cols[c]],
            rs1_s.at[p, st, d - 1, c], rs1_r.at[p, st, d - 1, c], xdev(d),
        )

    def rs0(p, st, d):
        return remote(
            p_ref.at[p, st, peer(d)], r0_ref.at[p, st, d - 1],
            rs0_s.at[p, st, d - 1], rs0_r.at[p, st, d - 1], xdev(d),
        )

    def rsz(p, st, c):
        return remote(
            zs_ref.at[p, st, :, cols[c]], zr_ref.at[p, st, :, cols[c]],
            rsz_s.at[p, st, c], rsz_r.at[p, st, c], zdev,
        )

    def mid(st):
        return remote(m1_ref.at[st], m2_ref.at[st], m_s.at[st], m_r.at[st], (s + step_of[st], e))

    def nslots(st):
        return remote(
            mys_ref.at[st], nbs_ref.at[st], n_s.at[st], n_r.at[st], (s - step_of[st], e)
        )

    def place(k, q_row, rows):
        pick = (q_row == slot_of_row(iota((2 * MAIN, tokens), 0), k)).astype(F32).astype(BF16)
        return dot(pick, rows)

    def pack(q_row, normed_of, dst):
        tail = jnp.zeros((MAIN, G), F32)
        for k in range(groups):
            placed = place(k, q_row, normed_of(k))
            dst[:, pl.ds(k * G, G)] = placed[:MAIN].astype(BF16)
            tail = tail + placed[MAIN:]
        dst[:, pl.ds(groups * G, G)] = tail.astype(BF16)

    def stats(load):
        ss = jnp.zeros((tokens, G), F32)
        xr = jnp.zeros((tokens, G), F32)
        for k in range(groups):
            v = load(k)
            ss = ss + v * v
            xr = xr + v * router_ref[:, pl.ds(k * G, G)]
        scale = lax.rsqrt(jnp.sum(ss, axis=1, keepdims=True) / width + EPS)
        affinity = jax.nn.sigmoid(scale * jnp.sum(xr, axis=1, keepdims=True))
        return scale, affinity

    def first(st):
        def load(k):
            return in_refs[st][0, :, pl.ds(k * G, G)].astype(F32)

        scale, affinity = stats(load)
        aff_ref[0, st] = jnp.broadcast_to(affinity, (tokens, 128))
        pack(
            slot_refs[st][0, 0], lambda k: (load(k) * scale).astype(BF16), g_ref.at[0, st, x]
        )

    def gate_up(p, st):
        blocks = 8 * MAIN
        tails = g_ref[p, st, :, :, pl.ds(groups * G, G)].reshape(blocks, G)
        r, c = iota((groups * MAIN, blocks), 0), iota((groups * MAIN, blocks), 1)
        sel = c == 16 * ((r >> 1) & 7) + 2 * (r >> 4) + (r & 1)
        tails = dot(sel.astype(F32).astype(BF16), tails).astype(BF16)
        acc = jnp.zeros((blocks + MAIN, wgu_ref.shape[1]), F32)
        for k in range(groups):
            rows = g_ref[p, st, :, :, pl.ds(k * G, G)].reshape(blocks, G)
            rows = jnp.concatenate([rows, tails[k * MAIN : (k + 1) * MAIN]], axis=0)
            acc = acc + dot(rows, wgu_ref[pl.ds(k * G, G), :])
        half = wgu_ref.shape[1] // 2
        gate, upper = acc[:, :half], acc[:, half:]
        return (gate * jax.nn.sigmoid(gate) * upper).astype(BF16)

    def down(p, st, hidden, tails, c):
        blocks = 8 * MAIN
        for k in range(*chunks[c]):
            if k < groups:
                out = dot(hidden, wd_ref[:, pl.ds(k * G, G)]).astype(BF16)
                p_ref[p, st, :, :, pl.ds(k * G, G)] = out[:blocks].reshape(8, MAIN, G)
                tails.append(out[blocks:])
            else:
                r, q = iota((blocks, groups * MAIN), 1), iota((blocks, groups * MAIN), 0)
                sel = q == 16 * ((r >> 1) & 7) + 2 * (r >> 4) + (r & 1)
                out = dot(sel.astype(F32).astype(BF16), jnp.concatenate(tails, axis=0))
                p_ref[p, st, :, :, pl.ds(groups * G, G)] = out.astype(BF16).reshape(8, MAIN, G)
        for d in (2, 1, 3):
            rs1(p, st, d, c).start()

    def reduce_other(p, st, c):
        for d in (1, 2, 3):
            rs1(p, st, d, c).wait_recv()
        total = p_ref[p, st, 4 + x, :, cols[c]].astype(F32)
        for d in (1, 2, 3):
            total = total + r1_ref[p, st, d - 1, :, cols[c]].astype(F32)
        zs_ref[p, st, :, cols[c]] = total.astype(BF16)
        rsz(p, st, c).start()

    def finish(p, st, load, store):
        for d in (1, 2, 3):
            rs0(p, st, d).wait_recv()
        for c in range(len(chunks)):
            rsz(p, st, c).wait_recv()

        def total(k):
            at = pl.ds(k * G, G)
            v = p_ref[p, st, x, :, at].astype(F32) + zr_ref[p, st, :, at].astype(F32)
            for d in (1, 2, 3):
                v = v + r0_ref[p, st, d - 1, :, at].astype(F32)
            high = v.astype(BF16)
            return high, (v - high.astype(F32)).astype(BF16)

        q_row = slot_refs[st][0, p].astype(F32)
        eye = iota((tokens, tokens), 0) == iota((tokens, tokens), 1)
        q_col = jnp.sum(jnp.where(eye, q_row, 0.0), axis=1, keepdims=True)
        affinity = aff_ref[p, st, :, 0:1]
        tail_high, tail_low = total(groups)
        for k in range(groups):
            high, low = total(k)
            lane = iota((tokens, 4 * MAIN), 1) & (2 * MAIN - 1)
            pick = (q_col == slot_of_row(lane, k).astype(F32)).astype(F32).astype(BF16)
            taken = dot(pick, jnp.concatenate([high, tail_high, low, tail_low], axis=0))
            store(k, (load(k) + affinity * taken).astype(BF16))

    def finish_first(st):
        squares = [jnp.zeros((tokens, G), F32)]

        def load(k):
            return in_refs[st][0, :, pl.ds(k * G, G)].astype(F32)

        def store(k, value):
            m1_ref[st, :, pl.ds(k * G, G)] = value
            value = value.astype(F32)
            squares[0] = squares[0] + value * value

        finish(0, st, load, store)
        scale = lax.rsqrt(jnp.sum(squares[0], axis=1, keepdims=True) / width + EPS)

        @pl.when(has_next[st])
        def _():
            nslots(st).wait_recv()

        def normed(k):
            return (m1_ref[st, :, pl.ds(k * G, G)].astype(F32) * scale).astype(BF16)

        pack(nbs_ref[st, 0:1, 0:tokens], normed, b2_ref.at[st])

        @pl.when(has_next[st])
        def _():
            for c in range(len(chunks)):
                agz(1, st, c).start()
            own(st).start()
            mid(st).start()

    def arrive_own(st):
        @pl.when(has_prev[st])
        def _():
            own(st).wait_recv()

        for d in (2, 1, 3):
            ago(1, st, d).start()

    def relay(p, st, c):
        if p == 0:
            agz(p, st, c).wait_recv()
        else:
            @pl.when(has_prev[st])
            def _():
                agz(p, st, c).wait_recv()
        for d in (2, 1, 3):
            agx(p, st, d, c).start()

    def gathered(p, st):
        for d in (1, 2, 3):
            ago(p, st, d).wait_recv()
            for c in range(len(chunks)):
                agx(p, st, d, c).wait_recv()

    def middle(st):
        @pl.when(has_prev[st])
        def _():
            mid(st).wait_recv()

        _, affinity = stats(lambda k: m2_ref[st, :, pl.ds(k * G, G)].astype(F32))
        aff_ref[1, st] = jnp.broadcast_to(affinity, (tokens, 128))

    def finish_second(st):
        def load(k):
            return m2_ref[st, :, pl.ds(k * G, G)].astype(F32)

        def store(k, value):
            out_refs[st][0, :, pl.ds(k * G, G)] = value

        finish(1, st, load, store)

    def sent_gather(p, st):
        def late():
            for c in range(len(chunks)):
                agz(p, st, c).wait_send()
            if p == 1:
                own(st).wait_send()
                mid(st).wait_send()

        if p == 0:
            late()
        else:
            pl.when(has_next[st])(late)
        for d in (1, 2, 3):
            ago(p, st, d).wait_send()
            for c in range(len(chunks)):
                agx(p, st, d, c).wait_send()

    def sent_reduce(p, st):
        for d in (1, 2, 3):
            rs0(p, st, d).wait_send()
            for c in range(len(chunks)):
                rs1(p, st, d, c).wait_send()
        for c in range(len(chunks)):
            rsz(p, st, c).wait_send()

    half = wg_hbm.shape[2]
    weights = [
        pltpu.make_async_copy(wg_hbm.at[0], wgu_ref.at[:, pl.ds(0, half)], w_sem.at[0]),
        pltpu.make_async_copy(wu_hbm.at[0], wgu_ref.at[:, pl.ds(half, half)], w_sem.at[1]),
        pltpu.make_async_copy(wd_hbm.at[0], wd_ref, w_sem.at[2]),
    ]
    for w in weights:
        w.start()

    barrier = pltpu.get_barrier_semaphore()

    def greet(device):
        pl.semaphore_signal(barrier, inc=1, device_id=device, device_id_type=MESH)

    greet(zdev)
    for d in (1, 2, 3):
        greet(xdev(d))
    for step in (1, -1):
        @pl.when((s + step >= 0) & (s + step < sections))
        def _(step=step):
            greet((s + step, e))
            greet((s + step, other))

    first(0)
    for st in (0, 1):
        mys_ref[st] = jnp.zeros(mys_ref.shape[1:], jnp.int32)
        mys_ref[st, 0:1, 0:tokens] = slot_refs[st][0, 1]

        @pl.when(jnp.logical_not(has_next[st]))
        def _(st=st):
            nbs_ref[st] = jnp.zeros(nbs_ref.shape[1:], jnp.int32)

        @pl.when(jnp.logical_not(has_prev[st]))
        def _(st=st):
            g_ref[1, st, x] = jnp.zeros(g_ref.shape[3:], BF16)
            g_ref[1, st, 4 + x] = jnp.zeros(g_ref.shape[3:], BF16)
            m2_ref[st] = jnp.zeros(m2_ref.shape[1:], BF16)

    neighbours = 4 + 2 * (s > 0).astype(jnp.int32) + 2 * (s < sections - 1).astype(jnp.int32)
    pl.semaphore_wait(barrier, neighbours)

    def send_first(st):
        for c in range(len(chunks)):
            agz(0, st, c).start()
        for d in (2, 1, 3):
            ago(0, st, d).start()

    send_first(0)
    first(1)
    send_first(1)
    for st in (0, 1):
        @pl.when(has_prev[st])
        def _(st=st):
            nslots(st).start()

    n = len(chunks)
    for p in (0, 1):
        for c in range(n):
            relay(p, 0, c)
        if p == 0:
            for w in weights:
                w.wait()
        gathered(p, 0)
        hidden = gate_up(p, 0)
        tails = []
        for c in range(n):
            down(p, 0, hidden, tails, c)
        for d in (2, 1, 3):
            rs0(p, 0, d).start()
        if p == 1:
            arrive_own(1)
        relay(p, 1, 0)
        relay(p, 1, 1)
        reduce_other(p, 0, 0)
        reduce_other(p, 0, 1)
        relay(p, 1, 2)
        reduce_other(p, 0, 2)
        relay(p, 1, 3)
        reduce_other(p, 0, 3)
        gathered(p, 1)
        hidden = gate_up(p, 1)
        tails = []
        for c in range(n):
            down(p, 1, hidden, tails, c)
        for d in (2, 1, 3):
            rs0(p, 1, d).start()
        for c in range(n):
            reduce_other(p, 1, c)
        if p == 0:
            finish_first(0)
            for st in (0, 1):
                sent_gather(0, st)
                sent_reduce(0, st)
                pl.when(has_prev[st])(lambda st=st: nslots(st).wait_send())
            finish_first(1)
            arrive_own(0)
            middle(0)
        else:
            middle(1)
            for st in (0, 1):
                sent_gather(1, st)
            finish_second(0)
            sent_reduce(1, 0)
            finish_second(1)
            sent_reduce(1, 1)


def shards(up_in, down_in, router, w_gate, w_up, w_down, slots_up, slots_down, *, sections):
    _, tokens, width = up_in.shape
    groups = width // G
    packed = width + G
    ends = [(groups + 1) * i // 4 for i in range(5)]
    chunks = list(zip(ends[:-1], ends[1:]))
    n = len(chunks)
    ffd = w_gate.shape[2]
    vmem = pl.BlockSpec(memory_space=pltpu.VMEM)
    hbm = pl.BlockSpec(memory_space=pl.ANY)
    dma = pltpu.SemaphoreType.DMA
    out = jax.ShapeDtypeStruct(up_in.shape, BF16)
    return pl.pallas_call(
        functools.partial(kernel_entry, chunks=chunks, sections=sections),
        name="relay_layers",
        out_shape=(out, out),
        in_specs=[vmem] * 5 + [hbm] * 3,
        out_specs=(vmem, vmem),
        scratch_shapes=[
            pltpu.VMEM((2, 2, 8, MAIN, packed), BF16),
            pltpu.VMEM((2, 2, 8, MAIN, packed), BF16),
            pltpu.VMEM((2, 2, 3, MAIN, packed), BF16),
            pltpu.VMEM((2, 2, 3, MAIN, packed), BF16),
            pltpu.VMEM((2, 2, MAIN, packed), BF16),
            pltpu.VMEM((2, 2, MAIN, packed), BF16),
            pltpu.VMEM((2, MAIN, packed), BF16),
            pltpu.VMEM((2, tokens, width), BF16),
            pltpu.VMEM((2, tokens, width), BF16),
            pltpu.VMEM((2, 2, tokens, 128), F32),
            pltpu.VMEM((2, 8, 128), jnp.int32),
            pltpu.VMEM((2, 8, 128), jnp.int32),
            pltpu.VMEM((width, 2 * ffd), BF16),
            pltpu.VMEM((ffd, width), BF16),
            dma((3,)),
            dma((2, 2, n)), dma((2, 2, n)),
            dma((2, 2, 3, n)), dma((2, 2, 3, n)),
            dma((2, 2, 3)), dma((2, 2, 3)),
            dma((2,)), dma((2,)),
            dma((2, 2, 3, n)), dma((2, 2, 3, n)),
            dma((2, 2, 3)), dma((2, 2, 3)),
            dma((2, 2, n)), dma((2, 2, n)),
            dma((2,)), dma((2,)),
            dma((2,)), dma((2,)),
        ],
        compiler_params=pltpu.CompilerParams(
            collective_id=0, has_side_effects=True, vmem_limit_bytes=48 * 1024 * 1024
        ),
    )(up_in, down_in, router, slots_up, slots_down, w_gate, w_up, w_down)


def kernel_entry(*refs, chunks, sections):
    kernel(*refs[:24], chunks, sections, *refs[24:])


def solution(mesh):
    in_specs = (
        P("section", "expert", None),
        P("section", "expert", None),
        P("section", None),
        P("section", None, "expert"),
        P("section", None, "expert"),
        P("section", "expert", None),
        P("section", None, "expert", None),
        P("section", None, "expert", None),
    )
    out_specs = (P("section", "expert", None), P("section", "expert", None))
    body = functools.partial(shards, sections=mesh.shape["section"])
    return jax.shard_map(body, mesh=mesh, in_specs=in_specs, out_specs=out_specs, check_vma=False)
```

```python
import functools

import jax
import jax.numpy as jnp
from jax import lax
from jax.experimental import pallas as pl
from jax.experimental.pallas import tpu as pltpu
from jax.sharding import PartitionSpec as P

MESH = pl.DeviceIdType.MESH
CAP = 18
MAIN = 16
G = 512
EPS = 1e-06
F32 = jnp.float32
BF16 = jnp.bfloat16


VMEM_LIMIT = 62 * 1024 * 1024
CHUNKS = 4
ORDER = [
    ("begin", 0),
    ("send_own", 0, 0),
    ("begin", 1),
    ("slots",),
    ("send_own", 0, 1),
    ("send_shift", 0),
    ("send_shift", 1),
    ("relay", 0, 0, 0),
    ("relay", 0, 0, 1),
    ("relay", 0, 0, 2),
    ("relay", 0, 0, 3),
    ("weights",),
    ("relay", 0, 1, 0),
    ("compute", 0, 0),
    ("relay", 0, 1, 1),
    ("reduce", 0, 0, 0),
    ("relay", 0, 1, 3),
    ("reduce", 0, 0, 1),
    ("relay", 0, 1, 2),
    ("reduce", 0, 0, 3),
    ("send_rows", 0, 0),
    ("reduce", 0, 0, 2),
    ("compute", 0, 1),
    ("send_rows", 0, 1),
    ("reduce", 0, 1, 1),
    ("reduce", 0, 1, 2),
    ("reduce", 0, 1, 3),
    ("reduce", 0, 1, 0),
    ("finish_first", 0),
    ("own", 0),
    ("finish_first", 1),
    ("relay", 1, 0, 0),
    ("relay", 1, 0, 1),
    ("relay", 1, 0, 2),
    ("own", 1),
    ("relay", 1, 0, 3),
    ("relay", 1, 1, 0),
    ("relay", 1, 1, 1),
    ("compute", 1, 0),
    ("reduce", 1, 0, 0),
    ("relay", 1, 1, 3),
    ("reduce", 1, 0, 2),
    ("reduce", 1, 0, 1),
    ("relay", 1, 1, 2),
    ("compute", 1, 1),
    ("slots_sent",),
    ("sent_gather", 0, 0),
    ("sent_gather", 0, 1),
    ("send_rows", 1, 1),
    ("reduce", 1, 0, 3),
    ("reduce", 1, 1, 0),
    ("reduce", 1, 1, 1),
    ("reduce", 1, 1, 2),
    ("reduce", 1, 1, 3),
    ("send_rows", 1, 0),
    ("sent_reduce", 0, 0),
    ("sent_reduce", 0, 1),
    ("sent_gather", 1, 0),
    ("sent_gather", 1, 1),
    ("finish_second", 0),
    ("finish_second", 1),
    ("sent_reduce", 1, 0),
    ("sent_reduce", 1, 1),
]


def iota(shape, axis):
    return lax.broadcasted_iota(jnp.int32, shape, axis)


def slot_of_row(row, k):
    tail = row - MAIN - 2 * k
    return jnp.where(
        row < MAIN, row, jnp.where((tail >= 0) & (tail < CAP - MAIN), MAIN + tail, -1)
    )


def dot(a, b):
    return jnp.dot(a, b, preferred_element_type=F32)


def kernel(
    up_hbm, dn_hbm, router_hbm, su_hbm, sd_hbm, wg_hbm, wu_hbm, wd_hbm,
    uo_ref, do_ref,
    x_ref, router_ref, slots_ref,
    g_ref, p_ref, r0_ref, r1_ref, zs_ref, zr_ref, b2_ref, m1_ref, m2_ref, dl_ref, dr_ref,
    aff_ref, mys_ref, nbs_ref, prs_ref, wgu_ref, wd_ref, chunks, sections,
    w_sem, agz_s, agz_r, agx_s, agx_r, ago_s, ago_r, own_s, own_r,
    rs1_s, rs1_r, rs0_s, rs0_r, rsz_s, rsz_r, m_s, m_r, n_s, n_r, o_s, o_r,
):
    s = lax.axis_index("section")
    e = lax.axis_index("expert")
    x = e // 2
    h = e % 2
    other = x * 2 + (1 - h)
    width = x_ref.shape[2]
    groups = width // G
    tokens = x_ref.shape[1]
    out_refs = (uo_ref, do_ref)
    n = len(chunks)
    cols = [pl.ds(a * G, (b - a) * G) for a, b in chunks]

    def peer(d):
        return lax.rem(x + d, 4)

    def xdev(d):
        return (s, peer(d) * 2 + h)

    zdev = (s, other)
    step_of = (1, -1)
    has_next = (s < sections - 1, s > 0)
    has_prev = (s > 0, s < sections - 1)

    def remote(src, dst, ssem, rsem, device):
        return pltpu.make_async_remote_copy(
            src_ref=src, dst_ref=dst, send_sem=ssem, recv_sem=rsem,
            device_id=device, device_id_type=MESH,
        )

    def agz(p, st, c):
        if p == 0:
            src, device = g_ref.at[p, st, x, :, cols[c]], zdev
        else:
            src, device = b2_ref.at[st, :, cols[c]], (s + step_of[st], other)
        return remote(
            src, g_ref.at[p, st, 4 + x, :, cols[c]],
            agz_s.at[p, st, c], agz_r.at[p, st, c], device,
        )

    def agx(p, st, d, c):
        blk = g_ref.at[p, st, 4 + x, :, cols[c]]
        return remote(blk, blk, agx_s.at[p, st, d - 1, c], agx_r.at[p, st, d - 1, c], xdev(d))

    def ago(p, st, d):
        blk = g_ref.at[p, st, x]
        return remote(blk, blk, ago_s.at[p, st, d - 1], ago_r.at[p, st, d - 1], xdev(d))

    def change(st):
        return remote(
            dl_ref.at[st], dr_ref.at[st], own_s.at[st], own_r.at[st], (s + step_of[st], e)
        )

    def rs1(p, st, d, c):
        return remote(
            p_ref.at[p, st, 4 + peer(d), :, cols[c]], r1_ref.at[p, st, d - 1, :, cols[c]],
            rs1_s.at[p, st, d - 1, c], rs1_r.at[p, st, d - 1, c], xdev(d),
        )

    def rs0(p, st, d):
        return remote(
            p_ref.at[p, st, peer(d)], r0_ref.at[p, st, d - 1],
            rs0_s.at[p, st, d - 1], rs0_r.at[p, st, d - 1], xdev(d),
        )

    def rsz(p, st, c):
        return remote(
            zs_ref.at[p, st, :, cols[c]], zr_ref.at[p, st, :, cols[c]],
            rsz_s.at[p, st, c], rsz_r.at[p, st, c], zdev,
        )

    def shift(st):
        return remote(x_ref.at[st], m2_ref.at[st], m_s.at[st], m_r.at[st], (s + step_of[st], e))

    def nslots(st):
        return remote(
            mys_ref.at[1, st], nbs_ref.at[st], n_s.at[st], n_r.at[st], (s - step_of[st], e)
        )

    def oslots(st):
        return remote(
            mys_ref.at[0, st], prs_ref.at[st], o_s.at[st], o_r.at[st], (s + step_of[st], e)
        )

    def place(k, q_row, rows):
        pick = (q_row == slot_of_row(iota((2 * MAIN, tokens), 0), k)).astype(F32).astype(BF16)
        return dot(pick, rows)

    def pack(q_row, normed_of, dst):
        tail = jnp.zeros((MAIN, G), F32)
        for k in range(groups):
            placed = place(k, q_row, normed_of(k))
            dst[:, pl.ds(k * G, G)] = placed[:MAIN].astype(BF16)
            tail = tail + placed[MAIN:]
        dst[:, pl.ds(groups * G, G)] = tail.astype(BF16)

    def stats(load):
        ss = jnp.zeros((tokens, G), F32)
        xr = jnp.zeros((tokens, G), F32)
        for k in range(groups):
            v = load(k)
            ss = ss + v * v
            xr = xr + v * router_ref[:, pl.ds(k * G, G)]
        scale = lax.rsqrt(jnp.sum(ss, axis=1, keepdims=True) / width + EPS)
        affinity = jax.nn.sigmoid(scale * jnp.sum(xr, axis=1, keepdims=True))
        return scale, affinity

    def first(st):
        def load(k):
            return x_ref[st, :, pl.ds(k * G, G)].astype(F32)

        scale, affinity = stats(load)
        aff_ref[0, st] = jnp.broadcast_to(affinity, (tokens, 128))
        pack(
            slots_ref[st, 0], lambda k: (load(k) * scale).astype(BF16), g_ref.at[0, st, x]
        )

    def gate_up(p, st):
        blocks = 8 * MAIN
        tails = g_ref[p, st, :, :, pl.ds(groups * G, G)].reshape(blocks, G)
        r, c = iota((groups * MAIN, blocks), 0), iota((groups * MAIN, blocks), 1)
        sel = c == 16 * ((r >> 1) & 7) + 2 * (r >> 4) + (r & 1)
        tails = dot(sel.astype(F32).astype(BF16), tails).astype(BF16)
        acc = jnp.zeros((blocks + MAIN, wgu_ref.shape[1]), F32)
        for k in range(groups):
            rows = g_ref[p, st, :, :, pl.ds(k * G, G)].reshape(blocks, G)
            rows = jnp.concatenate([rows, tails[k * MAIN : (k + 1) * MAIN]], axis=0)
            acc = acc + dot(rows, wgu_ref[pl.ds(k * G, G), :])
        half = wgu_ref.shape[1] // 2
        gate, upper = acc[:, :half], acc[:, half:]
        return (gate * jax.nn.sigmoid(gate) * upper).astype(BF16)

    def down(p, st, hidden, tails, c):
        blocks = 8 * MAIN
        for k in range(*chunks[c]):
            if k < groups:
                out = dot(hidden, wd_ref[:, pl.ds(k * G, G)]).astype(BF16)
                p_ref[p, st, :, :, pl.ds(k * G, G)] = out[:blocks].reshape(8, MAIN, G)
                tails.append(out[blocks:])
            else:
                r, q = iota((blocks, groups * MAIN), 1), iota((blocks, groups * MAIN), 0)
                sel = q == 16 * ((r >> 1) & 7) + 2 * (r >> 4) + (r & 1)
                out = dot(sel.astype(F32).astype(BF16), jnp.concatenate(tails, axis=0))
                p_ref[p, st, :, :, pl.ds(groups * G, G)] = out.astype(BF16).reshape(8, MAIN, G)
        for d in (2, 1, 3):
            rs1(p, st, d, c).start()

    def reduce_other(p, st, c):
        for d in (1, 2, 3):
            rs1(p, st, d, c).wait_recv()
        total = p_ref[p, st, 4 + x, :, cols[c]].astype(F32)
        for d in (1, 2, 3):
            total = total + r1_ref[p, st, d - 1, :, cols[c]].astype(F32)
        zs_ref[p, st, :, cols[c]] = total.astype(BF16)
        rsz(p, st, c).start()

    def column(q_row):
        eye = iota((tokens, tokens), 0) == iota((tokens, tokens), 1)
        return jnp.sum(jnp.where(eye, q_row.astype(F32), 0.0), axis=1, keepdims=True)

    def finish(p, st, load, store):
        for d in (1, 2, 3):
            rs0(p, st, d).wait_recv()
        for c in range(n):
            rsz(p, st, c).wait_recv()

        def total(k):
            at = pl.ds(k * G, G)
            v = p_ref[p, st, x, :, at].astype(F32) + zr_ref[p, st, :, at].astype(F32)
            for d in (1, 2, 3):
                v = v + r0_ref[p, st, d - 1, :, at].astype(F32)
            high = v.astype(BF16)
            return high, (v - high.astype(F32)).astype(BF16)

        q_col = column(slots_ref[st, p])
        affinity = aff_ref[p, st, :, 0:1]
        tail_high, tail_low = total(groups)
        for k in range(groups):
            high, low = total(k)
            lane = iota((tokens, 4 * MAIN), 1) & (2 * MAIN - 1)
            pick = (q_col == slot_of_row(lane, k).astype(F32)).astype(F32).astype(BF16)
            taken = dot(pick, jnp.concatenate([high, tail_high, low, tail_low], axis=0))
            store(k, (load(k) + affinity * taken).astype(BF16))

    def finish_first(st):
        squares = [jnp.zeros((tokens, G), F32)]
        tail = [jnp.zeros((MAIN, G), F32)]

        def load(k):
            return x_ref[st, :, pl.ds(k * G, G)].astype(F32)

        def store(k, value):
            m1_ref[st, :, pl.ds(k * G, G)] = value
            placed = place(k, slots_ref[st, 0], value)
            dl_ref[st, :, pl.ds(k * G, G)] = placed[:MAIN].astype(BF16)
            tail[0] = tail[0] + placed[MAIN:]
            value = value.astype(F32)
            squares[0] = squares[0] + value * value

        finish(0, st, load, store)
        dl_ref[st, :, pl.ds(groups * G, G)] = tail[0].astype(BF16)

        @pl.when(has_next[st])
        def _():
            change(st).start()
            nslots(st).wait_recv()

        scale = lax.rsqrt(jnp.sum(squares[0], axis=1, keepdims=True) / width + EPS)

        def normed(k):
            return (m1_ref[st, :, pl.ds(k * G, G)].astype(F32) * scale).astype(BF16)

        pack(nbs_ref[st, 0:1, 0:tokens], normed, b2_ref.at[st])

        @pl.when(has_next[st])
        def _():
            for c in range(n):
                agz(1, st, c).start()

    def send_shift(st):
        pl.when(has_next[st])(lambda: shift(st).start())

    def arrive_own(st):
        @pl.when(has_prev[st])
        def _():
            shift(st).wait_recv()
            oslots(st).wait_recv()
            change(st).wait_recv()

        q_col = column(prs_ref[st, 0:1, 0:tokens])
        kept = q_col >= float(CAP)
        tail = dr_ref[st, :, pl.ds(groups * G, G)]
        for k in range(groups):
            where = pl.ds(k * G, G)
            lane = iota((tokens, 2 * MAIN), 1)
            pick = (q_col == slot_of_row(lane, k).astype(F32)).astype(F32).astype(BF16)
            rows = dot(pick, jnp.concatenate([dr_ref[st, :, where], tail], axis=0))
            rows = jnp.where(kept, m2_ref[st, :, where].astype(F32), rows)
            m2_ref[st, :, where] = rows.astype(BF16)

        def load(k):
            return m2_ref[st, :, pl.ds(k * G, G)].astype(F32)

        scale, affinity = stats(load)
        aff_ref[1, st] = jnp.broadcast_to(affinity, (tokens, 128))
        pack(slots_ref[st, 1], lambda k: (load(k) * scale).astype(BF16), g_ref.at[1, st, x])
        send_own(1, st)

    def send_own(p, st):
        for d in (2, 1, 3):
            ago(p, st, d).start()

    def relay(p, st, c):
        if p == 0:
            agz(p, st, c).wait_recv()
        else:
            @pl.when(has_prev[st])
            def _():
                agz(p, st, c).wait_recv()
        for d in (2, 1, 3):
            agx(p, st, d, c).start()

    def gathered(p, st):
        for d in (1, 2, 3):
            ago(p, st, d).wait_recv()
            for c in range(n):
                agx(p, st, d, c).wait_recv()

    def finish_second(st):
        def load(k):
            return m2_ref[st, :, pl.ds(k * G, G)].astype(F32)

        def store(k, value):
            out_refs[st][0, :, pl.ds(k * G, G)] = value

        finish(1, st, load, store)

    def sent_gather(p, st):
        def late():
            for c in range(n):
                agz(p, st, c).wait_send()
            if p == 1:
                change(st).wait_send()
                shift(st).wait_send()

        if p == 0:
            late()
        else:
            pl.when(has_next[st])(late)
        for d in (1, 2, 3):
            ago(p, st, d).wait_send()
            for c in range(n):
                agx(p, st, d, c).wait_send()

    def sent_reduce(p, st):
        for d in (1, 2, 3):
            rs0(p, st, d).wait_send()
            for c in range(n):
                rs1(p, st, d, c).wait_send()
        for c in range(n):
            rsz(p, st, c).wait_send()

    barrier = pltpu.get_barrier_semaphore()

    def greet(device):
        pl.semaphore_signal(barrier, inc=1, device_id=device, device_id_type=MESH)

    greet(zdev)
    for d in (1, 2, 3):
        greet(xdev(d))
    for step in (1, -1):
        @pl.when((s + step >= 0) & (s + step < sections))
        def _(step=step):
            greet((s + step, e))
            greet((s + step, other))

    half = wg_hbm.shape[2]
    weights = [
        pltpu.make_async_copy(wg_hbm.at[0], wgu_ref.at[:, pl.ds(0, half)], w_sem.at[0]),
        pltpu.make_async_copy(wu_hbm.at[0], wgu_ref.at[:, pl.ds(half, half)], w_sem.at[1]),
        pltpu.make_async_copy(wd_hbm.at[0], wd_ref, w_sem.at[2]),
    ]
    loads = [
        pltpu.make_async_copy(up_hbm.at[0], x_ref.at[0], w_sem.at[3]),
        pltpu.make_async_copy(router_hbm, router_ref, w_sem.at[4]),
        pltpu.make_async_copy(su_hbm.at[0], slots_ref.at[0], w_sem.at[5]),
        pltpu.make_async_copy(sd_hbm.at[0], slots_ref.at[1], w_sem.at[6]),
        pltpu.make_async_copy(dn_hbm.at[0], x_ref.at[1], w_sem.at[7]),
    ]
    for copy in loads + weights:
        copy.start()

    for copy in loads[:4]:
        copy.wait()
    first(0)
    for st in (0, 1):
        for p in (0, 1):
            mys_ref[p, st] = jnp.zeros(mys_ref.shape[2:], jnp.int32)
            mys_ref[p, st, 0:1, 0:tokens] = slots_ref[st, p]

        @pl.when(jnp.logical_not(has_next[st]))
        def _(st=st):
            nbs_ref[st] = jnp.zeros(nbs_ref.shape[1:], jnp.int32)

        @pl.when(jnp.logical_not(has_prev[st]))
        def _(st=st):
            prs_ref[st] = jnp.zeros(prs_ref.shape[1:], jnp.int32)
            dr_ref[st] = jnp.zeros(dr_ref.shape[1:], BF16)
            g_ref[1, st, 4 + x] = jnp.zeros(g_ref.shape[3:], BF16)
            m2_ref[st] = jnp.zeros(m2_ref.shape[1:], BF16)

    neighbours = 4 + 2 * (s > 0).astype(jnp.int32) + 2 * (s < sections - 1).astype(jnp.int32)
    pl.semaphore_wait(barrier, neighbours)

    def begin(st):
        if st == 1:
            loads[4].wait()
            first(1)
        for c in range(n):
            agz(0, st, c).start()

    def slots():
        for st in (0, 1):
            @pl.when(has_prev[st])
            def _(st=st):
                nslots(st).start()

            @pl.when(has_next[st])
            def _(st=st):
                oslots(st).start()

    def slots_sent():
        for st in (0, 1):
            pl.when(has_prev[st])(lambda st=st: nslots(st).wait_send())
            pl.when(has_next[st])(lambda st=st: oslots(st).wait_send())

    def weights_here():
        for w in weights:
            w.wait()

    def compute(p, st):
        gathered(p, st)
        hidden = gate_up(p, st)
        tails = []
        for c in range(n):
            down(p, st, hidden, tails, c)

    def send_rows(p, st):
        for d in (2, 1, 3):
            rs0(p, st, d).start()

    steps = dict(
        begin=begin, send_own=send_own, slots=slots, slots_sent=slots_sent, weights=weights_here,
        relay=relay, own=arrive_own, compute=compute, send_rows=send_rows, reduce=reduce_other,
        finish_first=finish_first, send_shift=send_shift,
        finish_second=finish_second, sent_gather=sent_gather, sent_reduce=sent_reduce,
    )
    for name, *args in ORDER:
        steps[name](*args)


def shards(up_in, down_in, router, w_gate, w_up, w_down, slots_up, slots_down, *, sections):
    _, tokens, width = up_in.shape
    groups = width // G
    packed = width + G
    ends = [(groups + 1) * i // CHUNKS for i in range(CHUNKS + 1)]
    chunks = list(zip(ends[:-1], ends[1:]))
    n = len(chunks)
    ffd = w_gate.shape[2]
    vmem = pl.BlockSpec(memory_space=pltpu.VMEM)
    hbm = pl.BlockSpec(memory_space=pl.ANY)
    dma = pltpu.SemaphoreType.DMA
    out = jax.ShapeDtypeStruct(up_in.shape, BF16)
    return pl.pallas_call(
        functools.partial(kernel_entry, chunks=chunks, sections=sections),
        name="relay_layers",
        out_shape=(out, out),
        in_specs=[hbm] * 8,
        out_specs=(vmem, vmem),
        scratch_shapes=[
            pltpu.VMEM((2, tokens, width), BF16),
            pltpu.VMEM((1, width), F32),
            pltpu.VMEM((2, 2, 1, tokens), jnp.int32),
            pltpu.VMEM((2, 2, 8, MAIN, packed), BF16),
            pltpu.VMEM((2, 2, 8, MAIN, packed), BF16),
            pltpu.VMEM((2, 2, 3, MAIN, packed), BF16),
            pltpu.VMEM((2, 2, 3, MAIN, packed), BF16),
            pltpu.VMEM((2, 2, MAIN, packed), BF16),
            pltpu.VMEM((2, 2, MAIN, packed), BF16),
            pltpu.VMEM((2, MAIN, packed), BF16),
            pltpu.VMEM((2, tokens, width), BF16),
            pltpu.VMEM((2, tokens, width), BF16),
            pltpu.VMEM((2, MAIN, packed), BF16),
            pltpu.VMEM((2, MAIN, packed), BF16),
            pltpu.VMEM((2, 2, tokens, 128), F32),
            pltpu.VMEM((2, 2, 8, 128), jnp.int32),
            pltpu.VMEM((2, 8, 128), jnp.int32),
            pltpu.VMEM((2, 8, 128), jnp.int32),
            pltpu.VMEM((width, 2 * ffd), BF16),
            pltpu.VMEM((ffd, width), BF16),
            dma((8,)),
            dma((2, 2, n)), dma((2, 2, n)),
            dma((2, 2, 3, n)), dma((2, 2, 3, n)),
            dma((2, 2, 3)), dma((2, 2, 3)),
            dma((2,)), dma((2,)),
            dma((2, 2, 3, n)), dma((2, 2, 3, n)),
            dma((2, 2, 3)), dma((2, 2, 3)),
            dma((2, 2, n)), dma((2, 2, n)),
            dma((2,)), dma((2,)),
            dma((2,)), dma((2,)),
            dma((2,)), dma((2,)),
        ],
        compiler_params=pltpu.CompilerParams(
            collective_id=0, has_side_effects=True, vmem_limit_bytes=VMEM_LIMIT
        ),
    )(up_in, down_in, router, slots_up, slots_down, w_gate, w_up, w_down)


def kernel_entry(*refs, chunks, sections):
    kernel(*refs[:30], chunks, sections, *refs[30:])


def solution(mesh):
    in_specs = (
        P("section", "expert", None),
        P("section", "expert", None),
        P("section", None),
        P("section", None, "expert"),
        P("section", None, "expert"),
        P("section", "expert", None),
        P("section", None, "expert", None),
        P("section", None, "expert", None),
    )
    out_specs = (P("section", "expert", None), P("section", "expert", None))
    body = functools.partial(shards, sections=mesh.shape["section"])
    return jax.shard_map(body, mesh=mesh, in_specs=in_specs, out_specs=out_specs, check_vma=False)
```

```python
import functools

import jax
import jax.numpy as jnp
from jax import lax
from jax.experimental import pallas as pl
from jax.experimental.pallas import tpu as pltpu
from jax.sharding import PartitionSpec as P

MESH = pl.DeviceIdType.MESH
CAP = 18
MAIN = 16
G = 512
EPS = 1e-06
F32 = jnp.float32
BF16 = jnp.bfloat16


VMEM_LIMIT = 62 * 1024 * 1024
CHUNKS = 2
KEPT = 48
ORDER = [
    ("begin", 0),
    ("send_own", 0, 0),
    ("begin", 1),
    ("slots",),
    ("send_shift", 1),
    ("relay_own", 0, 0),
    ("send_shift", 0),
    ("send_own", 0, 1),
    ("relay", 0, 0, 0),
    ("relay_own", 0, 1),
    ("relay", 0, 0, 1),
    ("relay", 0, 1, 0),
    ("weights",),
    ("compute", 0, 0),
    ("relay", 0, 1, 1),
    ("reduce", 0, 0, 0),
    ("reduce", 0, 0, 1),
    ("send_rows", 0, 0),
    ("compute", 0, 1),
    ("send_rows", 0, 1),
    ("reduce", 0, 1, 0),
    ("reduce", 0, 1, 1),
    ("pass_rows", 0, 0),
    ("pass_rows", 0, 1),
    ("finish_first", 0),
    ("finish_first", 1),
    ("own", 0),
    ("relay_own", 1, 0),
    ("relay", 1, 0, 0),
    ("relay", 1, 0, 1),
    ("own", 1),
    ("compute", 1, 0),
    ("relay", 1, 1, 0),
    ("reduce", 1, 0, 1),
    ("reduce", 1, 0, 0),
    ("relay", 1, 1, 1),
    ("relay_own", 1, 1),
    ("compute", 1, 1),
    ("slots_sent",),
    ("sent_gather", 0, 0),
    ("sent_gather", 0, 1),
    ("send_rows", 1, 1),
    ("reduce", 1, 1, 0),
    ("reduce", 1, 1, 1),
    ("send_rows", 1, 0),
    ("sent_reduce", 0, 0),
    ("sent_reduce", 0, 1),
    ("pass_rows", 1, 1),
    ("pass_rows", 1, 0),
    ("sent_gather", 1, 0),
    ("sent_gather", 1, 1),
    ("finish_second", 0),
    ("finish_second", 1),
    ("sent_reduce", 1, 0),
    ("sent_reduce", 1, 1),
]


def iota(shape, axis):
    return lax.broadcasted_iota(jnp.int32, shape, axis)


def slot_of_row(row, k):
    tail = row - MAIN - 2 * k
    return jnp.where(
        row < MAIN, row, jnp.where((tail >= 0) & (tail < CAP - MAIN), MAIN + tail, -1)
    )


def dot(a, b):
    return jnp.dot(a, b, preferred_element_type=F32)


def kernel(
    up_hbm, dn_hbm, router_hbm, su_hbm, sd_hbm, wg_hbm, wu_hbm, wd_hbm,
    uo_ref, do_ref,
    x_ref, router_ref, slots_ref,
    g_ref, p_ref, ra_ref, sb_ref, rb_ref, rd_ref, r1_ref, xs_ref, xr_ref, zs_ref, zr_ref, b2_ref, m1_ref, m2_ref, dl_ref, dr_ref,
    aff_ref, mys_ref, nbs_ref, prs_ref, wgu_ref, wd_ref, chunks, sections,
    w_sem, agz_s, agz_r, agx_s, agx_r, ago_s, ago_r, agp_s, agp_r, own_s, own_r,
    rs1_s, rs1_r, rsa_s, rsa_r, rsb_s, rsb_r, rsd_s, rsd_r, rsz_s, rsz_r, m_s, m_r, n_s, n_r, o_s, o_r,
):
    s = lax.axis_index("section")
    e = lax.axis_index("expert")
    x = e // 2
    h = e % 2
    other = x * 2 + (1 - h)
    width = x_ref.shape[2]
    groups = width // G
    tokens = x_ref.shape[1]
    out_refs = (uo_ref, do_ref)
    n = len(chunks)
    cols = [pl.ds(a * G, (b - a) * G) for a, b in chunks]

    pieces = [pl.ds(0, groups // 2 * G), pl.ds(groups // 2 * G, (groups + 1 - groups // 2) * G)]

    def peer(d):
        return lax.rem(x + d % 4, 4)

    def way(c):
        return 1 if c == 0 else -1

    def xdev(d):
        return (s, peer(d) * 2 + h)

    zdev = (s, other)
    step_of = (1, -1)
    has_next = (s < sections - 1, s > 0)
    has_prev = (s > 0, s < sections - 1)

    def remote(src, dst, ssem, rsem, device):
        return pltpu.make_async_remote_copy(
            src_ref=src, dst_ref=dst, send_sem=ssem, recv_sem=rsem,
            device_id=device, device_id_type=MESH,
        )

    def agz(p, st, c):
        if p == 0:
            src, device = g_ref.at[p, st, x, :, cols[c]], zdev
        else:
            src, device = b2_ref.at[st, :, cols[c]], (s + step_of[st], other)
        return remote(
            src, g_ref.at[p, st, 4 + x, :, cols[c]],
            agz_s.at[p, st, c], agz_r.at[p, st, c], device,
        )

    def agx(p, st, d, c):
        blk = g_ref.at[p, st, 4 + x, :, cols[c]]
        return remote(blk, blk, agx_s.at[p, st, d - 1, c], agx_r.at[p, st, d - 1, c], xdev(d))

    def ago(p, st, d, c):
        blk = g_ref.at[p, st, x, :, pieces[c]]
        i = (d + 1) // 2
        return remote(blk, blk, ago_s.at[p, st, i, c], ago_r.at[p, st, i, c], xdev(d))

    def agp(p, st, c):
        blk = g_ref.at[p, st, peer(-way(c)), :, pieces[c]]
        return remote(blk, blk, agp_s.at[p, st, c], agp_r.at[p, st, c], xdev(way(c)))

    def change(st):
        return remote(
            dl_ref.at[st], dr_ref.at[st], own_s.at[st], own_r.at[st], (s + step_of[st], e)
        )

    def rs1(p, st, d, c):
        return remote(
            p_ref.at[p, st, 4 + peer(d), :, cols[c]], r1_ref.at[p, st, d - 1, :, cols[c]],
            rs1_s.at[p, st, d - 1, c], rs1_r.at[p, st, d - 1, c], xdev(d),
        )

    def rsa(p, st, c):
        return remote(
            p_ref.at[p, st, peer(2), :, pieces[c]], ra_ref.at[p, st, :, pieces[c]],
            rsa_s.at[p, st, c], rsa_r.at[p, st, c], xdev(way(c)),
        )

    def rsb(p, st, c):
        return remote(
            sb_ref.at[p, st, :, pieces[c]], rb_ref.at[p, st, :, pieces[c]],
            rsb_s.at[p, st, c], rsb_r.at[p, st, c], xdev(way(c)),
        )

    def rsd(p, st, c):
        return remote(
            p_ref.at[p, st, peer(-way(c)), :, pieces[c]], rd_ref.at[p, st, :, pieces[c]],
            rsd_s.at[p, st, c], rsd_r.at[p, st, c], xdev(-way(c)),
        )

    def rsz(p, st, c):
        return remote(
            zs_ref.at[p, st, :, cols[c]], zr_ref.at[p, st, :, cols[c]],
            rsz_s.at[p, st, c], rsz_r.at[p, st, c], zdev,
        )

    def shift(st):
        return remote(
            xs_ref.at[st], xr_ref.at[st], m_s.at[st], m_r.at[st], (s + step_of[st], e)
        )

    def nslots(st):
        return remote(
            mys_ref.at[1, st], nbs_ref.at[st], n_s.at[st], n_r.at[st], (s - step_of[st], e)
        )

    def oslots(st):
        return remote(
            mys_ref.at[0, st], prs_ref.at[st], o_s.at[st], o_r.at[st], (s + step_of[st], e)
        )

    def place(k, q_row, rows):
        pick = (q_row == slot_of_row(iota((2 * MAIN, tokens), 0), k)).astype(F32).astype(BF16)
        return dot(pick, rows)

    def pack(q_row, normed_of, dst):
        tail = jnp.zeros((MAIN, G), F32)
        for k in range(groups):
            placed = place(k, q_row, normed_of(k))
            dst[:, pl.ds(k * G, G)] = placed[:MAIN].astype(BF16)
            tail = tail + placed[MAIN:]
        dst[:, pl.ds(groups * G, G)] = tail.astype(BF16)

    def stats(load):
        ss = jnp.zeros((tokens, G), F32)
        xr = jnp.zeros((tokens, G), F32)
        for k in range(groups):
            v = load(k)
            ss = ss + v * v
            xr = xr + v * router_ref[:, pl.ds(k * G, G)]
        scale = lax.rsqrt(jnp.sum(ss, axis=1, keepdims=True) / width + EPS)
        affinity = jax.nn.sigmoid(scale * jnp.sum(xr, axis=1, keepdims=True))
        return scale, affinity

    def first(st):
        def load(k):
            return x_ref[st, :, pl.ds(k * G, G)].astype(F32)

        scale, affinity = stats(load)
        aff_ref[0, st] = jnp.broadcast_to(affinity, (tokens, 128))
        pack(
            slots_ref[st, 0], lambda k: (load(k) * scale).astype(BF16), g_ref.at[0, st, x]
        )

    def gate_up(p, st):
        blocks = 8 * MAIN
        tails = g_ref[p, st, :, :, pl.ds(groups * G, G)].reshape(blocks, G)
        r, c = iota((groups * MAIN, blocks), 0), iota((groups * MAIN, blocks), 1)
        sel = c == 16 * ((r >> 1) & 7) + 2 * (r >> 4) + (r & 1)
        tails = dot(sel.astype(F32).astype(BF16), tails).astype(BF16)
        acc = jnp.zeros((blocks + MAIN, wgu_ref.shape[1]), F32)
        for k in range(groups):
            rows = g_ref[p, st, :, :, pl.ds(k * G, G)].reshape(blocks, G)
            rows = jnp.concatenate([rows, tails[k * MAIN : (k + 1) * MAIN]], axis=0)
            acc = acc + dot(rows, wgu_ref[pl.ds(k * G, G), :])
        half = wgu_ref.shape[1] // 2
        gate, upper = acc[:, :half], acc[:, half:]
        return (gate * jax.nn.sigmoid(gate) * upper).astype(BF16)

    def down(p, st, hidden, tails, c):
        blocks = 8 * MAIN
        for k in range(*chunks[c]):
            if k < groups:
                out = dot(hidden, wd_ref[:, pl.ds(k * G, G)]).astype(BF16)
                p_ref[p, st, :, :, pl.ds(k * G, G)] = out[:blocks].reshape(8, MAIN, G)
                tails.append(out[blocks:])
            else:
                r, q = iota((blocks, groups * MAIN), 1), iota((blocks, groups * MAIN), 0)
                sel = q == 16 * ((r >> 1) & 7) + 2 * (r >> 4) + (r & 1)
                out = dot(sel.astype(F32).astype(BF16), jnp.concatenate(tails, axis=0))
                p_ref[p, st, :, :, pl.ds(groups * G, G)] = out.astype(BF16).reshape(8, MAIN, G)
        for d in (2, 1, 3):
            rs1(p, st, d, c).start()

    def reduce_other(p, st, c):
        for d in (1, 2, 3):
            rs1(p, st, d, c).wait_recv()
        total = p_ref[p, st, 4 + x, :, cols[c]].astype(F32)
        for d in (1, 2, 3):
            total = total + r1_ref[p, st, d - 1, :, cols[c]].astype(F32)
        zs_ref[p, st, :, cols[c]] = total.astype(BF16)
        rsz(p, st, c).start()

    def column(q_row):
        eye = iota((tokens, tokens), 0) == iota((tokens, tokens), 1)
        return jnp.sum(jnp.where(eye, q_row.astype(F32), 0.0), axis=1, keepdims=True)

    def finish(p, st, load, store):
        for c in (0, 1):
            rsd(p, st, c).wait_recv()
            rsb(p, st, c).wait_recv()
        for c in range(n):
            rsz(p, st, c).wait_recv()

        def total(k):
            at = pl.ds(k * G, G)
            v = p_ref[p, st, x, :, at].astype(F32) + zr_ref[p, st, :, at].astype(F32)
            v = v + rb_ref[p, st, :, at].astype(F32) + rd_ref[p, st, :, at].astype(F32)
            high = v.astype(BF16)
            return high, (v - high.astype(F32)).astype(BF16)

        q_col = column(slots_ref[st, p])
        affinity = aff_ref[p, st, :, 0:1]
        tail_high, tail_low = total(groups)
        for k in range(groups):
            high, low = total(k)
            lane = iota((tokens, 4 * MAIN), 1) & (2 * MAIN - 1)
            pick = (q_col == slot_of_row(lane, k).astype(F32)).astype(F32).astype(BF16)
            taken = dot(pick, jnp.concatenate([high, tail_high, low, tail_low], axis=0))
            store(k, (load(k) + affinity * taken).astype(BF16))

    def finish_first(st):
        squares = [jnp.zeros((tokens, G), F32)]
        tail = [jnp.zeros((MAIN, G), F32)]

        def load(k):
            return x_ref[st, :, pl.ds(k * G, G)].astype(F32)

        def store(k, value):
            m1_ref[st, :, pl.ds(k * G, G)] = value
            placed = place(k, slots_ref[st, 0], value)
            dl_ref[st, :, pl.ds(k * G, G)] = placed[:MAIN].astype(BF16)
            tail[0] = tail[0] + placed[MAIN:]
            value = value.astype(F32)
            squares[0] = squares[0] + value * value

        finish(0, st, load, store)
        dl_ref[st, :, pl.ds(groups * G, G)] = tail[0].astype(BF16)

        @pl.when(has_next[st])
        def _():
            change(st).start()
            nslots(st).wait_recv()

        scale = lax.rsqrt(jnp.sum(squares[0], axis=1, keepdims=True) / width + EPS)

        def normed(k):
            return (m1_ref[st, :, pl.ds(k * G, G)].astype(F32) * scale).astype(BF16)

        pack(nbs_ref[st, 0:1, 0:tokens], normed, b2_ref.at[st])

        @pl.when(has_next[st])
        def _():
            for c in range(n):
                agz(1, st, c).start()

    def send_shift(st):
        pick = (slots_ref[st, 0] == iota((KEPT, tokens), 0) + CAP).astype(F32).astype(BF16)
        for k in range(groups):
            where = pl.ds(k * G, G)
            xs_ref[st, :, where] = dot(pick, x_ref[st, :, where]).astype(BF16)
        pl.when(has_next[st])(lambda: shift(st).start())

    def arrive_own(st):
        @pl.when(has_prev[st])
        def _():
            shift(st).wait_recv()
            oslots(st).wait_recv()
            change(st).wait_recv()

        q_col = column(prs_ref[st, 0:1, 0:tokens])
        lane = iota((tokens, KEPT), 1) + CAP
        kept = (q_col == lane.astype(F32)).astype(F32).astype(BF16)
        tail = dr_ref[st, :, pl.ds(groups * G, G)]
        for k in range(groups):
            where = pl.ds(k * G, G)
            lane = iota((tokens, 2 * MAIN), 1)
            pick = (q_col == slot_of_row(lane, k).astype(F32)).astype(F32).astype(BF16)
            rows = dot(pick, jnp.concatenate([dr_ref[st, :, where], tail], axis=0))
            m2_ref[st, :, where] = (rows + dot(kept, xr_ref[st, :, where])).astype(BF16)

        def load(k):
            return m2_ref[st, :, pl.ds(k * G, G)].astype(F32)

        scale, affinity = stats(load)
        aff_ref[1, st] = jnp.broadcast_to(affinity, (tokens, 128))
        pack(slots_ref[st, 1], lambda k: (load(k) * scale).astype(BF16), g_ref.at[1, st, x])
        send_own(1, st)

    def send_own(p, st):
        for c in (0, 1):
            for d in (way(c), -way(c)):
                ago(p, st, d, c).start()

    def relay_own(p, st):
        for c in (0, 1):
            ago(p, st, way(c), c).wait_recv()
            agp(p, st, c).start()

    def relay(p, st, c):
        if p == 0:
            agz(p, st, c).wait_recv()
        else:
            @pl.when(has_prev[st])
            def _():
                agz(p, st, c).wait_recv()
        for d in (2, 1, 3):
            agx(p, st, d, c).start()

    def gathered(p, st):
        for c in (0, 1):
            ago(p, st, -way(c), c).wait_recv()
            agp(p, st, c).wait_recv()
        for d in (1, 2, 3):
            for c in range(n):
                agx(p, st, d, c).wait_recv()

    def finish_second(st):
        def load(k):
            return m2_ref[st, :, pl.ds(k * G, G)].astype(F32)

        def store(k, value):
            out_refs[st][0, :, pl.ds(k * G, G)] = value

        finish(1, st, load, store)

    def sent_gather(p, st):
        def late():
            for c in range(n):
                agz(p, st, c).wait_send()
            if p == 1:
                change(st).wait_send()
                shift(st).wait_send()

        if p == 0:
            late()
        else:
            pl.when(has_next[st])(late)
        for c in (0, 1):
            agp(p, st, c).wait_send()
            for d in (1, -1):
                ago(p, st, d, c).wait_send()
        for d in (1, 2, 3):
            for c in range(n):
                agx(p, st, d, c).wait_send()

    def sent_reduce(p, st):
        for c in (0, 1):
            rsa(p, st, c).wait_send()
            rsb(p, st, c).wait_send()
            rsd(p, st, c).wait_send()
        for d in (1, 2, 3):
            for c in range(n):
                rs1(p, st, d, c).wait_send()
        for c in range(n):
            rsz(p, st, c).wait_send()

    barrier = pltpu.get_barrier_semaphore()

    def greet(device):
        pl.semaphore_signal(barrier, inc=1, device_id=device, device_id_type=MESH)

    greet(zdev)
    for d in (1, 2, 3):
        greet(xdev(d))
    for step in (1, -1):
        @pl.when((s + step >= 0) & (s + step < sections))
        def _(step=step):
            greet((s + step, e))
            greet((s + step, other))

    half = wg_hbm.shape[2]
    weights = [
        pltpu.make_async_copy(wg_hbm.at[0], wgu_ref.at[:, pl.ds(0, half)], w_sem.at[0]),
        pltpu.make_async_copy(wu_hbm.at[0], wgu_ref.at[:, pl.ds(half, half)], w_sem.at[1]),
        pltpu.make_async_copy(wd_hbm.at[0], wd_ref, w_sem.at[2]),
    ]
    loads = [
        pltpu.make_async_copy(up_hbm.at[0], x_ref.at[0], w_sem.at[3]),
        pltpu.make_async_copy(router_hbm, router_ref, w_sem.at[4]),
        pltpu.make_async_copy(su_hbm.at[0], slots_ref.at[0], w_sem.at[5]),
        pltpu.make_async_copy(sd_hbm.at[0], slots_ref.at[1], w_sem.at[6]),
        pltpu.make_async_copy(dn_hbm.at[0], x_ref.at[1], w_sem.at[7]),
    ]
    for copy in loads + weights:
        copy.start()

    for copy in loads[:4]:
        copy.wait()
    first(0)
    for st in (0, 1):
        for p in (0, 1):
            mys_ref[p, st] = jnp.zeros(mys_ref.shape[2:], jnp.int32)
            mys_ref[p, st, 0:1, 0:tokens] = slots_ref[st, p]

        @pl.when(jnp.logical_not(has_next[st]))
        def _(st=st):
            nbs_ref[st] = jnp.zeros(nbs_ref.shape[1:], jnp.int32)

        @pl.when(jnp.logical_not(has_prev[st]))
        def _(st=st):
            prs_ref[st] = jnp.zeros(prs_ref.shape[1:], jnp.int32)
            dr_ref[st] = jnp.zeros(dr_ref.shape[1:], BF16)
            g_ref[1, st, 4 + x] = jnp.zeros(g_ref.shape[3:], BF16)
            xr_ref[st] = jnp.zeros(xr_ref.shape[1:], BF16)

    neighbours = 4 + 2 * (s > 0).astype(jnp.int32) + 2 * (s < sections - 1).astype(jnp.int32)
    pl.semaphore_wait(barrier, neighbours)

    def begin(st):
        if st == 1:
            loads[4].wait()
            first(1)
        for c in range(n):
            agz(0, st, c).start()

    def slots():
        for st in (0, 1):
            @pl.when(has_prev[st])
            def _(st=st):
                nslots(st).start()

            @pl.when(has_next[st])
            def _(st=st):
                oslots(st).start()

    def slots_sent():
        for st in (0, 1):
            pl.when(has_prev[st])(lambda st=st: nslots(st).wait_send())
            pl.when(has_next[st])(lambda st=st: oslots(st).wait_send())

    def weights_here():
        for w in weights:
            w.wait()

    def compute(p, st):
        gathered(p, st)
        hidden = gate_up(p, st)
        tails = []
        for c in range(n):
            down(p, st, hidden, tails, c)

    def send_rows(p, st):
        for c in (0, 1):
            rsa(p, st, c).start()
            rsd(p, st, c).start()

    def pass_rows(p, st):
        for c in (0, 1):
            rsa(p, st, c).wait_recv()
            total = p_ref[p, st, peer(way(c)), :, pieces[c]].astype(F32)
            total = total + ra_ref[p, st, :, pieces[c]].astype(F32)
            sb_ref[p, st, :, pieces[c]] = total.astype(BF16)
            rsb(p, st, c).start()

    steps = dict(
        begin=begin, send_own=send_own, slots=slots, slots_sent=slots_sent, weights=weights_here,
        relay=relay, own=arrive_own, compute=compute, send_rows=send_rows, pass_rows=pass_rows, relay_own=relay_own, reduce=reduce_other,
        finish_first=finish_first, send_shift=send_shift,
        finish_second=finish_second, sent_gather=sent_gather, sent_reduce=sent_reduce,
    )
    for name, *args in ORDER:
        steps[name](*args)


def shards(up_in, down_in, router, w_gate, w_up, w_down, slots_up, slots_down, *, sections):
    _, tokens, width = up_in.shape
    groups = width // G
    packed = width + G
    ends = [(groups + 1) * i // CHUNKS for i in range(CHUNKS + 1)]
    chunks = list(zip(ends[:-1], ends[1:]))
    n = len(chunks)
    ffd = w_gate.shape[2]
    vmem = pl.BlockSpec(memory_space=pltpu.VMEM)
    hbm = pl.BlockSpec(memory_space=pl.ANY)
    dma = pltpu.SemaphoreType.DMA
    out = jax.ShapeDtypeStruct(up_in.shape, BF16)
    return pl.pallas_call(
        functools.partial(kernel_entry, chunks=chunks, sections=sections),
        name="relay_layers",
        out_shape=(out, out),
        in_specs=[hbm] * 8,
        out_specs=(vmem, vmem),
        scratch_shapes=[
            pltpu.VMEM((2, tokens, width), BF16),
            pltpu.VMEM((1, width), F32),
            pltpu.VMEM((2, 2, 1, tokens), jnp.int32),
            pltpu.VMEM((2, 2, 8, MAIN, packed), BF16),
            pltpu.VMEM((2, 2, 8, MAIN, packed), BF16),
            pltpu.VMEM((2, 2, MAIN, packed), BF16),
            pltpu.VMEM((2, 2, MAIN, packed), BF16),
            pltpu.VMEM((2, 2, MAIN, packed), BF16),
            pltpu.VMEM((2, 2, MAIN, packed), BF16),
            pltpu.VMEM((2, 2, 3, MAIN, packed), BF16),
            pltpu.VMEM((2, KEPT, width), BF16),
            pltpu.VMEM((2, KEPT, width), BF16),
            pltpu.VMEM((2, 2, MAIN, packed), BF16),
            pltpu.VMEM((2, 2, MAIN, packed), BF16),
            pltpu.VMEM((2, MAIN, packed), BF16),
            pltpu.VMEM((2, tokens, width), BF16),
            pltpu.VMEM((2, tokens, width), BF16),
            pltpu.VMEM((2, MAIN, packed), BF16),
            pltpu.VMEM((2, MAIN, packed), BF16),
            pltpu.VMEM((2, 2, tokens, 128), F32),
            pltpu.VMEM((2, 2, 8, 128), jnp.int32),
            pltpu.VMEM((2, 8, 128), jnp.int32),
            pltpu.VMEM((2, 8, 128), jnp.int32),
            pltpu.VMEM((width, 2 * ffd), BF16),
            pltpu.VMEM((ffd, width), BF16),
            dma((8,)),
            dma((2, 2, n)), dma((2, 2, n)),
            dma((2, 2, 3, n)), dma((2, 2, 3, n)),
            dma((2, 2, 2, 2)), dma((2, 2, 2, 2)),
            dma((2, 2, 2)), dma((2, 2, 2)),
            dma((2,)), dma((2,)),
            dma((2, 2, 3, n)), dma((2, 2, 3, n)),
            dma((2, 2, 2)), dma((2, 2, 2)),
            dma((2, 2, 2)), dma((2, 2, 2)),
            dma((2, 2, 2)), dma((2, 2, 2)),
            dma((2, 2, n)), dma((2, 2, n)),
            dma((2,)), dma((2,)),
            dma((2,)), dma((2,)),
            dma((2,)), dma((2,)),
        ],
        compiler_params=pltpu.CompilerParams(
            collective_id=0, has_side_effects=True, vmem_limit_bytes=VMEM_LIMIT
        ),
    )(up_in, down_in, router, slots_up, slots_down, w_gate, w_up, w_down)


def kernel_entry(*refs, chunks, sections):
    kernel(*refs[:35], chunks, sections, *refs[35:])


def solution(mesh):
    in_specs = (
        P("section", "expert", None),
        P("section", "expert", None),
        P("section", None),
        P("section", None, "expert"),
        P("section", None, "expert"),
        P("section", "expert", None),
        P("section", None, "expert", None),
        P("section", None, "expert", None),
    )
    out_specs = (P("section", "expert", None), P("section", "expert", None))
    body = functools.partial(shards, sections=mesh.shape["section"])
    return jax.shard_map(body, mesh=mesh, in_specs=in_specs, out_specs=out_specs, check_vma=False)
```

```python
import functools

import jax
import jax.numpy as jnp
from jax import lax
from jax.experimental import pallas as pl
from jax.experimental.pallas import tpu as pltpu
from jax.sharding import PartitionSpec as P

MESH = pl.DeviceIdType.MESH
CAP = 18
MAIN = 16
G = 512
EPS = 1e-06
F32 = jnp.float32
BF16 = jnp.bfloat16


VMEM_LIMIT = 62 * 1024 * 1024
CHUNKS = 4
KEPT = 48
ORDER = [
    ("begin", 0),
    ("send_own", 0, 0),
    ("begin", 1),
    ("slots",),
    ("relay", 0, 0, 0),
    ("send_shift", 0),
    ("send_own", 0, 1),
    ("send_shift", 1),
    ("relay", 0, 0, 1),
    ("relay_own", 0, 0),
    ("relay", 0, 0, 2),
    ("relay", 0, 0, 3),
    ("relay", 0, 1, 0),
    ("weights",),
    ("compute", 0, 0),
    ("relay", 0, 1, 1),
    ("reduce", 0, 0, 1),
    ("relay", 0, 1, 3),
    ("reduce", 0, 0, 2),
    ("relay", 0, 1, 2),
    ("reduce", 0, 0, 3),
    ("relay_own", 0, 1),
    ("reduce", 0, 0, 0),
    ("send_rows", 0, 0),
    ("compute", 0, 1),
    ("reduce", 0, 1, 0),
    ("reduce", 0, 1, 1),
    ("reduce", 0, 1, 3),
    ("reduce", 0, 1, 2),
    ("pass_rows", 0, 0),
    ("send_rows", 0, 1),
    ("pass_rows", 0, 1),
    ("finish_first", 0),
    ("own", 0),
    ("finish_first", 1),
    ("relay", 1, 0, 0),
    ("relay", 1, 0, 1),
    ("relay_own", 1, 0),
    ("relay", 1, 0, 2),
    ("relay", 1, 0, 3),
    ("own", 1),
    ("relay", 1, 1, 0),
    ("compute", 1, 0),
    ("relay", 1, 1, 1),
    ("relay", 1, 1, 2),
    ("reduce", 1, 0, 1),
    ("relay", 1, 1, 3),
    ("reduce", 1, 0, 2),
    ("reduce", 1, 0, 3),
    ("reduce", 1, 0, 0),
    ("relay_own", 1, 1),
    ("compute", 1, 1),
    ("slots_sent",),
    ("sent_gather", 0, 0),
    ("sent_gather", 0, 1),
    ("reduce", 1, 1, 0),
    ("send_rows", 1, 1),
    ("reduce", 1, 1, 1),
    ("reduce", 1, 1, 3),
    ("reduce", 1, 1, 2),
    ("send_rows", 1, 0),
    ("sent_reduce", 0, 0),
    ("sent_reduce", 0, 1),
    ("pass_rows", 1, 1),
    ("pass_rows", 1, 0),
    ("sent_gather", 1, 0),
    ("sent_gather", 1, 1),
    ("finish_second", 0),
    ("finish_second", 1),
    ("sent_reduce", 1, 0),
    ("sent_reduce", 1, 1),
]


def iota(shape, axis):
    return lax.broadcasted_iota(jnp.int32, shape, axis)


def slot_of_row(row, k):
    tail = row - MAIN - 2 * k
    return jnp.where(
        row < MAIN, row, jnp.where((tail >= 0) & (tail < CAP - MAIN), MAIN + tail, -1)
    )


def dot(a, b):
    return jnp.dot(a, b, preferred_element_type=F32)


def kernel(
    up_hbm, dn_hbm, router_hbm, su_hbm, sd_hbm, wg_hbm, wu_hbm, wd_hbm,
    uo_ref, do_ref,
    x_ref, router_ref, slots_ref,
    g_ref, p_ref, ra_ref, sb_ref, rb_ref, rd_ref, r1_ref, xs_ref, xr_ref, zs_ref, zr_ref, b2_ref, m1_ref, m2_ref, dl_ref, dr_ref,
    aff_ref, mys_ref, nbs_ref, prs_ref, wgu_ref, wd_ref, chunks, sections,
    w_sem, agz_s, agz_r, agx_s, agx_r, ago_s, ago_r, agp_s, agp_r, own_s, own_r,
    rs1_s, rs1_r, rsa_s, rsa_r, rsb_s, rsb_r, rsd_s, rsd_r, rsz_s, rsz_r, m_s, m_r, n_s, n_r, o_s, o_r,
):
    s = lax.axis_index("section")
    e = lax.axis_index("expert")
    x = e // 2
    h = e % 2
    other = x * 2 + (1 - h)
    width = x_ref.shape[2]
    groups = width // G
    tokens = x_ref.shape[1]
    out_refs = (uo_ref, do_ref)
    n = len(chunks)
    cols = [pl.ds(a * G, (b - a) * G) for a, b in chunks]

    pieces = [pl.ds(0, groups // 2 * G), pl.ds(groups // 2 * G, (groups + 1 - groups // 2) * G)]

    def peer(d):
        return lax.rem(x + d % 4, 4)

    def way(c):
        return 1 if c == 0 else -1

    def xdev(d):
        return (s, peer(d) * 2 + h)

    zdev = (s, other)
    step_of = (1, -1)
    has_next = (s < sections - 1, s > 0)
    has_prev = (s > 0, s < sections - 1)

    def remote(src, dst, ssem, rsem, device):
        return pltpu.make_async_remote_copy(
            src_ref=src, dst_ref=dst, send_sem=ssem, recv_sem=rsem,
            device_id=device, device_id_type=MESH,
        )

    def agz(p, st, c):
        if p == 0:
            src, device = g_ref.at[p, st, x, :, cols[c]], zdev
        else:
            src, device = b2_ref.at[st, :, cols[c]], (s + step_of[st], other)
        return remote(
            src, g_ref.at[p, st, 4 + x, :, cols[c]],
            agz_s.at[p, st, c], agz_r.at[p, st, c], device,
        )

    def agx(p, st, d, c):
        blk = g_ref.at[p, st, 4 + x, :, cols[c]]
        return remote(blk, blk, agx_s.at[p, st, d - 1, c], agx_r.at[p, st, d - 1, c], xdev(d))

    def ago(p, st, d, c):
        blk = g_ref.at[p, st, x, :, pieces[c]]
        i = (d + 1) // 2
        return remote(blk, blk, ago_s.at[p, st, i, c], ago_r.at[p, st, i, c], xdev(d))

    def agp(p, st, c):
        blk = g_ref.at[p, st, peer(-way(c)), :, pieces[c]]
        return remote(blk, blk, agp_s.at[p, st, c], agp_r.at[p, st, c], xdev(way(c)))

    def change(st):
        return remote(
            dl_ref.at[st], dr_ref.at[st], own_s.at[st], own_r.at[st], (s + step_of[st], e)
        )

    def rs1(p, st, d, c):
        return remote(
            p_ref.at[p, st, 4 + peer(d), :, cols[c]], r1_ref.at[p, st, d - 1, :, cols[c]],
            rs1_s.at[p, st, d - 1, c], rs1_r.at[p, st, d - 1, c], xdev(d),
        )

    def rsa(p, st, c):
        return remote(
            p_ref.at[p, st, peer(2), :, pieces[c]], ra_ref.at[p, st, :, pieces[c]],
            rsa_s.at[p, st, c], rsa_r.at[p, st, c], xdev(way(c)),
        )

    def rsb(p, st, c):
        return remote(
            sb_ref.at[p, st, :, pieces[c]], rb_ref.at[p, st, :, pieces[c]],
            rsb_s.at[p, st, c], rsb_r.at[p, st, c], xdev(way(c)),
        )

    def rsd(p, st, c):
        return remote(
            p_ref.at[p, st, peer(-way(c)), :, pieces[c]], rd_ref.at[p, st, :, pieces[c]],
            rsd_s.at[p, st, c], rsd_r.at[p, st, c], xdev(-way(c)),
        )

    def rsz(p, st, c):
        return remote(
            zs_ref.at[p, st, :, cols[c]], zr_ref.at[p, st, :, cols[c]],
            rsz_s.at[p, st, c], rsz_r.at[p, st, c], zdev,
        )

    def shift(st):
        return remote(
            xs_ref.at[st], xr_ref.at[st], m_s.at[st], m_r.at[st], (s + step_of[st], e)
        )

    def nslots(st):
        return remote(
            mys_ref.at[1, st], nbs_ref.at[st], n_s.at[st], n_r.at[st], (s - step_of[st], e)
        )

    def oslots(st):
        return remote(
            mys_ref.at[0, st], prs_ref.at[st], o_s.at[st], o_r.at[st], (s + step_of[st], e)
        )

    def place(k, q_row, rows):
        pick = (q_row == slot_of_row(iota((2 * MAIN, tokens), 0), k)).astype(F32).astype(BF16)
        return dot(pick, rows)

    def pack(q_row, normed_of, dst):
        tail = jnp.zeros((MAIN, G), F32)
        for k in range(groups):
            placed = place(k, q_row, normed_of(k))
            dst[:, pl.ds(k * G, G)] = placed[:MAIN].astype(BF16)
            tail = tail + placed[MAIN:]
        dst[:, pl.ds(groups * G, G)] = tail.astype(BF16)

    def stats(load):
        ss = jnp.zeros((tokens, G), F32)
        xr = jnp.zeros((tokens, G), F32)
        for k in range(groups):
            v = load(k)
            ss = ss + v * v
            xr = xr + v * router_ref[:, pl.ds(k * G, G)]
        scale = lax.rsqrt(jnp.sum(ss, axis=1, keepdims=True) / width + EPS)
        affinity = jax.nn.sigmoid(scale * jnp.sum(xr, axis=1, keepdims=True))
        return scale, affinity

    def first(st):
        def load(k):
            return x_ref[st, :, pl.ds(k * G, G)].astype(F32)

        scale, affinity = stats(load)
        aff_ref[0, st] = jnp.broadcast_to(affinity, (tokens, 128))
        pack(
            slots_ref[st, 0], lambda k: (load(k) * scale).astype(BF16), g_ref.at[0, st, x]
        )

    def gate_up(p, st):
        blocks = 8 * MAIN
        tails = g_ref[p, st, :, :, pl.ds(groups * G, G)].reshape(blocks, G)
        r, c = iota((groups * MAIN, blocks), 0), iota((groups * MAIN, blocks), 1)
        sel = c == 16 * ((r >> 1) & 7) + 2 * (r >> 4) + (r & 1)
        tails = dot(sel.astype(F32).astype(BF16), tails).astype(BF16)
        acc = jnp.zeros((blocks + MAIN, wgu_ref.shape[1]), F32)
        for k in range(groups):
            rows = g_ref[p, st, :, :, pl.ds(k * G, G)].reshape(blocks, G)
            rows = jnp.concatenate([rows, tails[k * MAIN : (k + 1) * MAIN]], axis=0)
            acc = acc + dot(rows, wgu_ref[pl.ds(k * G, G), :])
        half = wgu_ref.shape[1] // 2
        gate, upper = acc[:, :half], acc[:, half:]
        return (gate * jax.nn.sigmoid(gate) * upper).astype(BF16)

    def down(p, st, hidden, tails, c):
        blocks = 8 * MAIN
        for k in range(*chunks[c]):
            if k < groups:
                out = dot(hidden, wd_ref[:, pl.ds(k * G, G)]).astype(BF16)
                p_ref[p, st, :, :, pl.ds(k * G, G)] = out[:blocks].reshape(8, MAIN, G)
                tails.append(out[blocks:])
            else:
                r, q = iota((blocks, groups * MAIN), 1), iota((blocks, groups * MAIN), 0)
                sel = q == 16 * ((r >> 1) & 7) + 2 * (r >> 4) + (r & 1)
                out = dot(sel.astype(F32).astype(BF16), jnp.concatenate(tails, axis=0))
                p_ref[p, st, :, :, pl.ds(groups * G, G)] = out.astype(BF16).reshape(8, MAIN, G)
        for d in (2, 1, 3):
            rs1(p, st, d, c).start()

    def reduce_other(p, st, c):
        for d in (1, 2, 3):
            rs1(p, st, d, c).wait_recv()
        total = p_ref[p, st, 4 + x, :, cols[c]].astype(F32)
        for d in (1, 2, 3):
            total = total + r1_ref[p, st, d - 1, :, cols[c]].astype(F32)
        zs_ref[p, st, :, cols[c]] = total.astype(BF16)
        rsz(p, st, c).start()

    def column(q_row):
        eye = iota((tokens, tokens), 0) == iota((tokens, tokens), 1)
        return jnp.sum(jnp.where(eye, q_row.astype(F32), 0.0), axis=1, keepdims=True)

    def finish(p, st, load, store):
        for c in (0, 1):
            rsd(p, st, c).wait_recv()
            rsb(p, st, c).wait_recv()
        for c in range(n):
            rsz(p, st, c).wait_recv()

        def total(k):
            at = pl.ds(k * G, G)
            v = p_ref[p, st, x, :, at].astype(F32) + zr_ref[p, st, :, at].astype(F32)
            v = v + rb_ref[p, st, :, at].astype(F32) + rd_ref[p, st, :, at].astype(F32)
            high = v.astype(BF16)
            return high, (v - high.astype(F32)).astype(BF16)

        q_col = column(slots_ref[st, p])
        affinity = aff_ref[p, st, :, 0:1]
        tail_high, tail_low = total(groups)
        for k in range(groups):
            high, low = total(k)
            lane = iota((tokens, 4 * MAIN), 1) & (2 * MAIN - 1)
            pick = (q_col == slot_of_row(lane, k).astype(F32)).astype(F32).astype(BF16)
            taken = dot(pick, jnp.concatenate([high, tail_high, low, tail_low], axis=0))
            store(k, (load(k) + affinity * taken).astype(BF16))

    def finish_first(st):
        squares = [jnp.zeros((tokens, G), F32)]
        tail = [jnp.zeros((MAIN, G), F32)]

        def load(k):
            return x_ref[st, :, pl.ds(k * G, G)].astype(F32)

        def store(k, value):
            m1_ref[st, :, pl.ds(k * G, G)] = value
            placed = place(k, slots_ref[st, 0], value)
            dl_ref[st, :, pl.ds(k * G, G)] = placed[:MAIN].astype(BF16)
            tail[0] = tail[0] + placed[MAIN:]
            value = value.astype(F32)
            squares[0] = squares[0] + value * value

        finish(0, st, load, store)
        dl_ref[st, :, pl.ds(groups * G, G)] = tail[0].astype(BF16)

        @pl.when(has_next[st])
        def _():
            change(st).start()
            nslots(st).wait_recv()

        scale = lax.rsqrt(jnp.sum(squares[0], axis=1, keepdims=True) / width + EPS)

        def normed(k):
            return (m1_ref[st, :, pl.ds(k * G, G)].astype(F32) * scale).astype(BF16)

        pack(nbs_ref[st, 0:1, 0:tokens], normed, b2_ref.at[st])

        @pl.when(has_next[st])
        def _():
            for c in range(n):
                agz(1, st, c).start()

    def send_shift(st):
        pick = (slots_ref[st, 0] == iota((KEPT, tokens), 0) + CAP).astype(F32).astype(BF16)
        for k in range(groups):
            where = pl.ds(k * G, G)
            xs_ref[st, :, where] = dot(pick, x_ref[st, :, where]).astype(BF16)
        pl.when(has_next[st])(lambda: shift(st).start())

    def arrive_own(st):
        @pl.when(has_prev[st])
        def _():
            shift(st).wait_recv()
            oslots(st).wait_recv()
            change(st).wait_recv()

        q_col = column(prs_ref[st, 0:1, 0:tokens])
        lane = iota((tokens, KEPT), 1) + CAP
        kept = (q_col == lane.astype(F32)).astype(F32).astype(BF16)
        tail = dr_ref[st, :, pl.ds(groups * G, G)]
        for k in range(groups):
            where = pl.ds(k * G, G)
            lane = iota((tokens, 2 * MAIN), 1)
            pick = (q_col == slot_of_row(lane, k).astype(F32)).astype(F32).astype(BF16)
            rows = dot(pick, jnp.concatenate([dr_ref[st, :, where], tail], axis=0))
            m2_ref[st, :, where] = (rows + dot(kept, xr_ref[st, :, where])).astype(BF16)

        def load(k):
            return m2_ref[st, :, pl.ds(k * G, G)].astype(F32)

        scale, affinity = stats(load)
        aff_ref[1, st] = jnp.broadcast_to(affinity, (tokens, 128))
        pack(slots_ref[st, 1], lambda k: (load(k) * scale).astype(BF16), g_ref.at[1, st, x])
        send_own(1, st)

    def send_own(p, st):
        for c in (0, 1):
            for d in (way(c), -way(c)):
                ago(p, st, d, c).start()

    def relay_own(p, st):
        for c in (0, 1):
            ago(p, st, way(c), c).wait_recv()
            agp(p, st, c).start()

    def relay(p, st, c):
        if p == 0:
            agz(p, st, c).wait_recv()
        else:
            @pl.when(has_prev[st])
            def _():
                agz(p, st, c).wait_recv()
        for d in (2, 1, 3):
            agx(p, st, d, c).start()

    def gathered(p, st):
        for c in (0, 1):
            ago(p, st, -way(c), c).wait_recv()
            agp(p, st, c).wait_recv()
        for d in (1, 2, 3):
            for c in range(n):
                agx(p, st, d, c).wait_recv()

    def result(st):
        return pltpu.make_async_copy(m2_ref.at[st], out_refs[st].at[0], w_sem.at[8 + st])

    def finish_second(st):
        def load(k):
            return m2_ref[st, :, pl.ds(k * G, G)].astype(F32)

        def store(k, value):
            m2_ref[st, :, pl.ds(k * G, G)] = value

        finish(1, st, load, store)
        result(st).start()

    def sent_gather(p, st):
        def late():
            for c in range(n):
                agz(p, st, c).wait_send()
            if p == 1:
                change(st).wait_send()
                shift(st).wait_send()

        if p == 0:
            late()
        else:
            pl.when(has_next[st])(late)
        for c in (0, 1):
            agp(p, st, c).wait_send()
            for d in (1, -1):
                ago(p, st, d, c).wait_send()
        for d in (1, 2, 3):
            for c in range(n):
                agx(p, st, d, c).wait_send()

    def sent_reduce(p, st):
        for c in (0, 1):
            rsa(p, st, c).wait_send()
            rsb(p, st, c).wait_send()
            rsd(p, st, c).wait_send()
        for d in (1, 2, 3):
            for c in range(n):
                rs1(p, st, d, c).wait_send()
        for c in range(n):
            rsz(p, st, c).wait_send()

    barrier = pltpu.get_barrier_semaphore()

    def greet(device):
        pl.semaphore_signal(barrier, inc=1, device_id=device, device_id_type=MESH)

    greet(zdev)
    for d in (1, 2, 3):
        greet(xdev(d))
    for step in (1, -1):
        @pl.when((s + step >= 0) & (s + step < sections))
        def _(step=step):
            greet((s + step, e))
            greet((s + step, other))

    half = wg_hbm.shape[2]
    weights = [
        pltpu.make_async_copy(wg_hbm.at[0], wgu_ref.at[:, pl.ds(0, half)], w_sem.at[0]),
        pltpu.make_async_copy(wu_hbm.at[0], wgu_ref.at[:, pl.ds(half, half)], w_sem.at[1]),
        pltpu.make_async_copy(wd_hbm.at[0], wd_ref, w_sem.at[2]),
    ]
    loads = [
        pltpu.make_async_copy(up_hbm.at[0], x_ref.at[0], w_sem.at[3]),
        pltpu.make_async_copy(router_hbm, router_ref, w_sem.at[4]),
        pltpu.make_async_copy(su_hbm.at[0], slots_ref.at[0], w_sem.at[5]),
        pltpu.make_async_copy(sd_hbm.at[0], slots_ref.at[1], w_sem.at[6]),
        pltpu.make_async_copy(dn_hbm.at[0], x_ref.at[1], w_sem.at[7]),
    ]
    for copy in loads + weights:
        copy.start()

    for copy in loads[:4]:
        copy.wait()
    first(0)
    for st in (0, 1):
        for p in (0, 1):
            mys_ref[p, st] = jnp.zeros(mys_ref.shape[2:], jnp.int32)
            mys_ref[p, st, 0:1, 0:tokens] = slots_ref[st, p]

        @pl.when(jnp.logical_not(has_next[st]))
        def _(st=st):
            nbs_ref[st] = jnp.zeros(nbs_ref.shape[1:], jnp.int32)

        @pl.when(jnp.logical_not(has_prev[st]))
        def _(st=st):
            prs_ref[st] = jnp.zeros(prs_ref.shape[1:], jnp.int32)
            dr_ref[st] = jnp.zeros(dr_ref.shape[1:], BF16)
            g_ref[1, st, 4 + x] = jnp.zeros(g_ref.shape[3:], BF16)
            xr_ref[st] = jnp.zeros(xr_ref.shape[1:], BF16)

    neighbours = 4 + 2 * (s > 0).astype(jnp.int32) + 2 * (s < sections - 1).astype(jnp.int32)
    pl.semaphore_wait(barrier, neighbours)

    def begin(st):
        if st == 1:
            loads[4].wait()
            first(1)
        for c in range(n):
            agz(0, st, c).start()

    def slots():
        for st in (0, 1):
            @pl.when(has_prev[st])
            def _(st=st):
                nslots(st).start()

            @pl.when(has_next[st])
            def _(st=st):
                oslots(st).start()

    def slots_sent():
        for st in (0, 1):
            pl.when(has_prev[st])(lambda st=st: nslots(st).wait_send())
            pl.when(has_next[st])(lambda st=st: oslots(st).wait_send())

    def weights_here():
        for w in weights:
            w.wait()

    def compute(p, st):
        gathered(p, st)
        hidden = gate_up(p, st)
        tails = []
        for c in range(n):
            down(p, st, hidden, tails, c)

    def send_rows(p, st):
        for c in (0, 1):
            rsa(p, st, c).start()
            rsd(p, st, c).start()

    def pass_rows(p, st):
        for c in (0, 1):
            rsa(p, st, c).wait_recv()
            total = p_ref[p, st, peer(way(c)), :, pieces[c]].astype(F32)
            total = total + ra_ref[p, st, :, pieces[c]].astype(F32)
            sb_ref[p, st, :, pieces[c]] = total.astype(BF16)
            rsb(p, st, c).start()

    steps = dict(
        begin=begin, send_own=send_own, slots=slots, slots_sent=slots_sent, weights=weights_here,
        relay=relay, own=arrive_own, compute=compute, send_rows=send_rows, pass_rows=pass_rows, relay_own=relay_own, reduce=reduce_other,
        finish_first=finish_first, send_shift=send_shift,
        finish_second=finish_second, sent_gather=sent_gather, sent_reduce=sent_reduce,
    )
    for name, *args in ORDER:
        steps[name](*args)
    for st in (0, 1):
        result(st).wait()


def shards(up_in, down_in, router, w_gate, w_up, w_down, slots_up, slots_down, *, sections):
    _, tokens, width = up_in.shape
    groups = width // G
    packed = width + G
    ends = [(groups + 1) * i // CHUNKS for i in range(CHUNKS + 1)]
    chunks = list(zip(ends[:-1], ends[1:]))
    n = len(chunks)
    ffd = w_gate.shape[2]
    hbm = pl.BlockSpec(memory_space=pl.ANY)
    dma = pltpu.SemaphoreType.DMA
    out = jax.ShapeDtypeStruct(up_in.shape, BF16)
    return pl.pallas_call(
        functools.partial(kernel_entry, chunks=chunks, sections=sections),
        name="relay_layers",
        out_shape=(out, out),
        in_specs=[hbm] * 8,
        out_specs=(hbm, hbm),
        scratch_shapes=[
            pltpu.VMEM((2, tokens, width), BF16),
            pltpu.VMEM((1, width), F32),
            pltpu.VMEM((2, 2, 1, tokens), jnp.int32),
            pltpu.VMEM((2, 2, 8, MAIN, packed), BF16),
            pltpu.VMEM((2, 2, 8, MAIN, packed), BF16),
            pltpu.VMEM((2, 2, MAIN, packed), BF16),
            pltpu.VMEM((2, 2, MAIN, packed), BF16),
            pltpu.VMEM((2, 2, MAIN, packed), BF16),
            pltpu.VMEM((2, 2, MAIN, packed), BF16),
            pltpu.VMEM((2, 2, 3, MAIN, packed), BF16),
            pltpu.VMEM((2, KEPT, width), BF16),
            pltpu.VMEM((2, KEPT, width), BF16),
            pltpu.VMEM((2, 2, MAIN, packed), BF16),
            pltpu.VMEM((2, 2, MAIN, packed), BF16),
            pltpu.VMEM((2, MAIN, packed), BF16),
            pltpu.VMEM((2, tokens, width), BF16),
            pltpu.VMEM((2, tokens, width), BF16),
            pltpu.VMEM((2, MAIN, packed), BF16),
            pltpu.VMEM((2, MAIN, packed), BF16),
            pltpu.VMEM((2, 2, tokens, 128), F32),
            pltpu.VMEM((2, 2, 8, 128), jnp.int32),
            pltpu.VMEM((2, 8, 128), jnp.int32),
            pltpu.VMEM((2, 8, 128), jnp.int32),
            pltpu.VMEM((width, 2 * ffd), BF16),
            pltpu.VMEM((ffd, width), BF16),
            dma((10,)),
            dma((2, 2, n)), dma((2, 2, n)),
            dma((2, 2, 3, n)), dma((2, 2, 3, n)),
            dma((2, 2, 2, 2)), dma((2, 2, 2, 2)),
            dma((2, 2, 2)), dma((2, 2, 2)),
            dma((2,)), dma((2,)),
            dma((2, 2, 3, n)), dma((2, 2, 3, n)),
            dma((2, 2, 2)), dma((2, 2, 2)),
            dma((2, 2, 2)), dma((2, 2, 2)),
            dma((2, 2, 2)), dma((2, 2, 2)),
            dma((2, 2, n)), dma((2, 2, n)),
            dma((2,)), dma((2,)),
            dma((2,)), dma((2,)),
            dma((2,)), dma((2,)),
        ],
        compiler_params=pltpu.CompilerParams(
            collective_id=0, has_side_effects=True, vmem_limit_bytes=VMEM_LIMIT
        ),
    )(up_in, down_in, router, slots_up, slots_down, w_gate, w_up, w_down)


def kernel_entry(*refs, chunks, sections):
    kernel(*refs[:35], chunks, sections, *refs[35:])


def solution(mesh):
    in_specs = (
        P("section", "expert", None),
        P("section", "expert", None),
        P("section", None),
        P("section", None, "expert"),
        P("section", None, "expert"),
        P("section", "expert", None),
        P("section", None, "expert", None),
        P("section", None, "expert", None),
    )
    out_specs = (P("section", "expert", None), P("section", "expert", None))
    body = functools.partial(shards, sections=mesh.shape["section"])
    return jax.shard_map(body, mesh=mesh, in_specs=in_specs, out_specs=out_specs, check_vma=False)
```

```python
import functools

import jax
import jax.numpy as jnp
from jax import lax
from jax.experimental import pallas as pl
from jax.experimental.pallas import tpu as pltpu
from jax.sharding import PartitionSpec as P

MESH = pl.DeviceIdType.MESH
CAP = 18
MAIN = 16
G = 512
EPS = 1e-06
F32 = jnp.float32
BF16 = jnp.bfloat16


VMEM_LIMIT = 62 * 1024 * 1024
CHUNKS = 4
KEPT = 48
ORDER = [
    ("begin", 0),
    ("send_own", 0, 0),
    ("begin", 1),
    ("slots",),
    ("relay", 0, 0, 0),
    ("send_shift", 0),
    ("send_own", 0, 1),
    ("send_shift", 1),
    ("relay", 0, 0, 1),
    ("relay_own", 0, 0),
    ("relay", 0, 0, 2),
    ("relay", 0, 0, 3),
    ("relay", 0, 1, 0),
    ("weights",),
    ("compute", 0, 0),
    ("relay", 0, 1, 1),
    ("reduce", 0, 0, 1),
    ("relay", 0, 1, 3),
    ("reduce", 0, 0, 2),
    ("relay", 0, 1, 2),
    ("reduce", 0, 0, 3),
    ("relay_own", 0, 1),
    ("reduce", 0, 0, 0),
    ("send_rows", 0, 0),
    ("compute", 0, 1),
    ("reduce", 0, 1, 0),
    ("reduce", 0, 1, 1),
    ("reduce", 0, 1, 3),
    ("reduce", 0, 1, 2),
    ("pass_rows", 0, 0),
    ("send_rows", 0, 1),
    ("pass_rows", 0, 1),
    ("finish_first", 0),
    ("own", 0),
    ("finish_first", 1),
    ("relay", 1, 0, 0),
    ("relay", 1, 0, 1),
    ("relay_own", 1, 0),
    ("relay", 1, 0, 2),
    ("relay", 1, 0, 3),
    ("own", 1),
    ("relay", 1, 1, 0),
    ("compute", 1, 0),
    ("relay", 1, 1, 1),
    ("relay", 1, 1, 2),
    ("reduce", 1, 0, 1),
    ("relay", 1, 1, 3),
    ("reduce", 1, 0, 2),
    ("reduce", 1, 0, 3),
    ("reduce", 1, 0, 0),
    ("relay_own", 1, 1),
    ("compute", 1, 1),
    ("slots_sent",),
    ("sent_gather", 0, 0),
    ("sent_gather", 0, 1),
    ("reduce", 1, 1, 0),
    ("send_rows", 1, 1),
    ("reduce", 1, 1, 1),
    ("reduce", 1, 1, 3),
    ("reduce", 1, 1, 2),
    ("send_rows", 1, 0),
    ("sent_reduce", 0, 0),
    ("sent_reduce", 0, 1),
    ("pass_rows", 1, 1),
    ("pass_rows", 1, 0),
    ("sent_gather", 1, 0),
    ("sent_gather", 1, 1),
    ("finish_second", 0),
    ("finish_second", 1),
    ("sent_reduce", 1, 0),
    ("sent_reduce", 1, 1),
]


def iota(shape, axis):
    return lax.broadcasted_iota(jnp.int32, shape, axis)


def slot_of_row(row, k):
    tail = row - MAIN - 2 * k
    return jnp.where(
        row < MAIN, row, jnp.where((tail >= 0) & (tail < CAP - MAIN), MAIN + tail, -1)
    )


def dot(a, b):
    return jnp.dot(a, b, preferred_element_type=F32)


def kernel(
    up_hbm, dn_hbm, router_hbm, su_hbm, sd_hbm, wg_hbm, wu_hbm, wd_hbm,
    uo_ref, do_ref,
    x_ref, router_ref, slots_ref,
    g_ref, p_ref, ra_ref, sb_ref, rb_ref, rd_ref, r1_ref, xs_ref, xr_ref, zs_ref, zr_ref, b2_ref, m1_ref, m2_ref, dl_ref, dr_ref,
    aff_ref, mys_ref, nbs_ref, prs_ref, wgu_ref, wd_ref, chunks, sections,
    w_sem, agz_s, agz_r, agx_s, agx_r, ago_s, ago_r, agp_s, agp_r, own_s, own_r,
    rs1_s, rs1_r, rsa_s, rsa_r, rsb_s, rsb_r, rsd_s, rsd_r, rsz_s, rsz_r, m_s, m_r, n_s, n_r, o_s, o_r,
):
    s = lax.axis_index("section")
    e = lax.axis_index("expert")
    x = e // 2
    h = e % 2
    other = x * 2 + (1 - h)
    width = x_ref.shape[2]
    groups = width // G
    tokens = x_ref.shape[1]
    out_refs = (uo_ref, do_ref)
    n = len(chunks)
    cols = [pl.ds(a * G, (b - a) * G) for a, b in chunks]

    pieces = [pl.ds(0, groups // 2 * G), pl.ds(groups // 2 * G, (groups + 1 - groups // 2) * G)]

    def peer(d):
        return lax.rem(x + d % 4, 4)

    def way(c):
        return 1 if c == 0 else -1

    def xdev(d):
        return (s, peer(d) * 2 + h)

    zdev = (s, other)
    step_of = (1, -1)
    has_next = (s < sections - 1, s > 0)
    has_prev = (s > 0, s < sections - 1)

    def remote(src, dst, ssem, rsem, device):
        return pltpu.make_async_remote_copy(
            src_ref=src, dst_ref=dst, send_sem=ssem, recv_sem=rsem,
            device_id=device, device_id_type=MESH,
        )

    def agz(p, st, c):
        if p == 0:
            src, device = g_ref.at[p, st, x, :, cols[c]], zdev
        else:
            src, device = b2_ref.at[st, :, cols[c]], (s + step_of[st], other)
        return remote(
            src, g_ref.at[p, st, 4 + x, :, cols[c]],
            agz_s.at[p, st, c], agz_r.at[p, st, c], device,
        )

    def agx(p, st, d, c):
        blk = g_ref.at[p, st, 4 + x, :, cols[c]]
        return remote(blk, blk, agx_s.at[p, st, d - 1, c], agx_r.at[p, st, d - 1, c], xdev(d))

    def ago(p, st, d, c):
        blk = g_ref.at[p, st, x, :, pieces[c]]
        i = (d + 1) // 2
        return remote(blk, blk, ago_s.at[p, st, i, c], ago_r.at[p, st, i, c], xdev(d))

    def agp(p, st, c):
        blk = g_ref.at[p, st, peer(-way(c)), :, pieces[c]]
        return remote(blk, blk, agp_s.at[p, st, c], agp_r.at[p, st, c], xdev(way(c)))

    def change(st):
        return remote(
            dl_ref.at[st], dr_ref.at[st], own_s.at[st], own_r.at[st], (s + step_of[st], e)
        )

    def rs1(p, st, d, c):
        return remote(
            p_ref.at[p, st, 4 + peer(d), :, cols[c]], r1_ref.at[p, st, d - 1, :, cols[c]],
            rs1_s.at[p, st, d - 1, c], rs1_r.at[p, st, d - 1, c], xdev(d),
        )

    def rsa(p, st, c):
        return remote(
            p_ref.at[p, st, peer(2), :, pieces[c]], ra_ref.at[p, st, :, pieces[c]],
            rsa_s.at[p, st, c], rsa_r.at[p, st, c], xdev(way(c)),
        )

    def rsb(p, st, c):
        return remote(
            sb_ref.at[p, st, :, pieces[c]], rb_ref.at[p, st, :, pieces[c]],
            rsb_s.at[p, st, c], rsb_r.at[p, st, c], xdev(way(c)),
        )

    def rsd(p, st, c):
        return remote(
            p_ref.at[p, st, peer(-way(c)), :, pieces[c]], rd_ref.at[p, st, :, pieces[c]],
            rsd_s.at[p, st, c], rsd_r.at[p, st, c], xdev(-way(c)),
        )

    def rsz(p, st, c):
        return remote(
            zs_ref.at[p, st, :, cols[c]], zr_ref.at[p, st, :, cols[c]],
            rsz_s.at[p, st, c], rsz_r.at[p, st, c], zdev,
        )

    def shift(st):
        return remote(
            xs_ref.at[st], xr_ref.at[st], m_s.at[st], m_r.at[st], (s + step_of[st], e)
        )

    def nslots(st):
        return remote(
            mys_ref.at[1, st], nbs_ref.at[st], n_s.at[st], n_r.at[st], (s - step_of[st], e)
        )

    def oslots(st):
        return remote(
            mys_ref.at[0, st], prs_ref.at[st], o_s.at[st], o_r.at[st], (s + step_of[st], e)
        )

    def place(k, q_row, rows):
        pick = (q_row == slot_of_row(iota((2 * MAIN, tokens), 0), k)).astype(F32).astype(BF16)
        return dot(pick, rows)

    def pack(q_row, normed_of, dst):
        tail = jnp.zeros((MAIN, G), F32)
        for k in range(groups):
            placed = place(k, q_row, normed_of(k))
            dst[:, pl.ds(k * G, G)] = placed[:MAIN].astype(BF16)
            tail = tail + placed[MAIN:]
        dst[:, pl.ds(groups * G, G)] = tail.astype(BF16)

    def stats(load):
        ss = jnp.zeros((tokens, G), F32)
        xr = jnp.zeros((tokens, G), F32)
        for k in range(groups):
            v = load(k)
            ss = ss + v * v
            xr = xr + v * router_ref[:, pl.ds(k * G, G)]
        scale = lax.rsqrt(jnp.sum(ss, axis=1, keepdims=True) / width + EPS)
        affinity = jax.nn.sigmoid(scale * jnp.sum(xr, axis=1, keepdims=True))
        return scale, affinity

    def first(st):
        def load(k):
            return x_ref[st, :, pl.ds(k * G, G)].astype(F32)

        scale, affinity = stats(load)
        aff_ref[0, st] = jnp.broadcast_to(affinity, (tokens, 128))
        pack(
            slots_ref[st, 0], lambda k: (load(k) * scale).astype(BF16), g_ref.at[0, st, x]
        )

    def gate_up(p, st):
        blocks = 8 * MAIN
        tails = g_ref[p, st, :, :, pl.ds(groups * G, G)].reshape(blocks, G)
        r, c = iota((groups * MAIN, blocks), 0), iota((groups * MAIN, blocks), 1)
        sel = c == 16 * ((r >> 1) & 7) + 2 * (r >> 4) + (r & 1)
        tails = dot(sel.astype(F32).astype(BF16), tails).astype(BF16)
        acc = jnp.zeros((blocks + MAIN, wgu_ref.shape[1]), F32)
        for k in range(groups):
            rows = g_ref[p, st, :, :, pl.ds(k * G, G)].reshape(blocks, G)
            rows = jnp.concatenate([rows, tails[k * MAIN : (k + 1) * MAIN]], axis=0)
            acc = acc + dot(rows, wgu_ref[pl.ds(k * G, G), :])
        half = wgu_ref.shape[1] // 2
        gate, upper = acc[:, :half], acc[:, half:]
        return (gate * jax.nn.sigmoid(gate) * upper).astype(BF16)

    def down(p, st, hidden, tails, c):
        blocks = 8 * MAIN
        for k in range(*chunks[c]):
            if k < groups:
                out = dot(hidden, wd_ref[:, pl.ds(k * G, G)]).astype(BF16)
                p_ref[p, st, :, :, pl.ds(k * G, G)] = out[:blocks].reshape(8, MAIN, G)
                tails.append(out[blocks:])
            else:
                r, q = iota((blocks, groups * MAIN), 1), iota((blocks, groups * MAIN), 0)
                sel = q == 16 * ((r >> 1) & 7) + 2 * (r >> 4) + (r & 1)
                out = dot(sel.astype(F32).astype(BF16), jnp.concatenate(tails, axis=0))
                p_ref[p, st, :, :, pl.ds(groups * G, G)] = out.astype(BF16).reshape(8, MAIN, G)
        for d in (2, 1, 3):
            rs1(p, st, d, c).start()

    def reduce_other(p, st, c):
        for d in (1, 2, 3):
            rs1(p, st, d, c).wait_recv()
        total = p_ref[p, st, 4 + x, :, cols[c]].astype(F32)
        for d in (1, 2, 3):
            total = total + r1_ref[p, st, d - 1, :, cols[c]].astype(F32)
        zs_ref[p, st, :, cols[c]] = total.astype(BF16)
        rsz(p, st, c).start()

    def column(q_row):
        eye = iota((tokens, tokens), 0) == iota((tokens, tokens), 1)
        return jnp.sum(jnp.where(eye, q_row.astype(F32), 0.0), axis=1, keepdims=True)

    def finish(p, st, load, store):
        for c in (0, 1):
            rsd(p, st, c).wait_recv()
            rsb(p, st, c).wait_recv()
        for c in range(n):
            rsz(p, st, c).wait_recv()

        def total(k):
            at = pl.ds(k * G, G)
            v = p_ref[p, st, x, :, at].astype(F32) + zr_ref[p, st, :, at].astype(F32)
            v = v + rb_ref[p, st, :, at].astype(F32) + rd_ref[p, st, :, at].astype(F32)
            high = v.astype(BF16)
            return high, (v - high.astype(F32)).astype(BF16)

        q_col = column(slots_ref[st, p])
        affinity = aff_ref[p, st, :, 0:1]
        tail_high, tail_low = total(groups)
        for k in range(groups):
            high, low = total(k)
            lane = iota((tokens, 4 * MAIN), 1) & (2 * MAIN - 1)
            pick = (q_col == slot_of_row(lane, k).astype(F32)).astype(F32).astype(BF16)
            taken = dot(pick, jnp.concatenate([high, tail_high, low, tail_low], axis=0))
            store(k, (load(k) + affinity * taken).astype(BF16))

    def finish_first(st):
        squares = [jnp.zeros((tokens, G), F32)]
        tail = [jnp.zeros((MAIN, G), F32)]

        def load(k):
            return x_ref[st, :, pl.ds(k * G, G)].astype(F32)

        def store(k, value):
            m1_ref[st, :, pl.ds(k * G, G)] = value
            placed = place(k, slots_ref[st, 0], value)
            dl_ref[st, :, pl.ds(k * G, G)] = placed[:MAIN].astype(BF16)
            tail[0] = tail[0] + placed[MAIN:]
            value = value.astype(F32)
            squares[0] = squares[0] + value * value

        finish(0, st, load, store)
        dl_ref[st, :, pl.ds(groups * G, G)] = tail[0].astype(BF16)

        @pl.when(has_next[st])
        def _():
            change(st).start()
            nslots(st).wait_recv()

        scale = lax.rsqrt(jnp.sum(squares[0], axis=1, keepdims=True) / width + EPS)

        def normed(k):
            return (m1_ref[st, :, pl.ds(k * G, G)].astype(F32) * scale).astype(BF16)

        pack(nbs_ref[st, 0:1, 0:tokens], normed, b2_ref.at[st])

        @pl.when(has_next[st])
        def _():
            for c in range(n):
                agz(1, st, c).start()

    def send_shift(st):
        pick = (slots_ref[st, 0] == iota((KEPT, tokens), 0) + CAP).astype(F32).astype(BF16)
        for k in range(groups):
            where = pl.ds(k * G, G)
            xs_ref[st, :, where] = dot(pick, x_ref[st, :, where]).astype(BF16)
        pl.when(has_next[st])(lambda: shift(st).start())

    def arrive_own(st):
        @pl.when(has_prev[st])
        def _():
            shift(st).wait_recv()
            oslots(st).wait_recv()
            change(st).wait_recv()

        q_col = column(prs_ref[st, 0:1, 0:tokens])
        lane = iota((tokens, KEPT), 1) + CAP
        kept = (q_col == lane.astype(F32)).astype(F32).astype(BF16)
        tail = dr_ref[st, :, pl.ds(groups * G, G)]
        for k in range(groups):
            where = pl.ds(k * G, G)
            lane = iota((tokens, 2 * MAIN), 1)
            pick = (q_col == slot_of_row(lane, k).astype(F32)).astype(F32).astype(BF16)
            rows = dot(pick, jnp.concatenate([dr_ref[st, :, where], tail], axis=0))
            m2_ref[st, :, where] = (rows + dot(kept, xr_ref[st, :, where])).astype(BF16)

        def load(k):
            return m2_ref[st, :, pl.ds(k * G, G)].astype(F32)

        scale, affinity = stats(load)
        aff_ref[1, st] = jnp.broadcast_to(affinity, (tokens, 128))
        pack(slots_ref[st, 1], lambda k: (load(k) * scale).astype(BF16), g_ref.at[1, st, x])
        send_own(1, st)

    def send_own(p, st):
        for c in (0, 1):
            for d in (way(c), -way(c)):
                ago(p, st, d, c).start()

    def relay_own(p, st):
        for c in (0, 1):
            ago(p, st, way(c), c).wait_recv()
            agp(p, st, c).start()

    def relay(p, st, c):
        if p == 0:
            agz(p, st, c).wait_recv()
        else:
            @pl.when(has_prev[st])
            def _():
                agz(p, st, c).wait_recv()
        for d in (2, 1, 3):
            agx(p, st, d, c).start()

    def gathered(p, st):
        for c in (0, 1):
            ago(p, st, -way(c), c).wait_recv()
            agp(p, st, c).wait_recv()
        for d in (1, 2, 3):
            for c in range(n):
                agx(p, st, d, c).wait_recv()

    def result(st):
        return pltpu.make_async_copy(m2_ref.at[st], out_refs[st].at[0], w_sem.at[8 + st])

    def finish_second(st):
        def load(k):
            return m2_ref[st, :, pl.ds(k * G, G)].astype(F32)

        def store(k, value):
            m2_ref[st, :, pl.ds(k * G, G)] = value

        finish(1, st, load, store)
        result(st).start()

    def sent_gather(p, st):
        def late():
            for c in range(n):
                agz(p, st, c).wait_send()
            if p == 1:
                change(st).wait_send()
                shift(st).wait_send()

        if p == 0:
            late()
        else:
            pl.when(has_next[st])(late)
        for c in (0, 1):
            agp(p, st, c).wait_send()
            for d in (1, -1):
                ago(p, st, d, c).wait_send()
        for d in (1, 2, 3):
            for c in range(n):
                agx(p, st, d, c).wait_send()

    def sent_reduce(p, st):
        for c in (0, 1):
            rsa(p, st, c).wait_send()
            rsb(p, st, c).wait_send()
            rsd(p, st, c).wait_send()
        for d in (1, 2, 3):
            for c in range(n):
                rs1(p, st, d, c).wait_send()
        for c in range(n):
            rsz(p, st, c).wait_send()

    barrier = pltpu.get_barrier_semaphore()

    def greet(device):
        pl.semaphore_signal(barrier, inc=1, device_id=device, device_id_type=MESH)

    greet(zdev)
    for d in (1, 2, 3):
        greet(xdev(d))
    for step in (1, -1):
        @pl.when((s + step >= 0) & (s + step < sections))
        def _(step=step):
            greet((s + step, e))
            greet((s + step, other))

    half = wg_hbm.shape[2]
    weights = [
        pltpu.make_async_copy(wg_hbm.at[0], wgu_ref.at[:, pl.ds(0, half)], w_sem.at[0]),
        pltpu.make_async_copy(wu_hbm.at[0], wgu_ref.at[:, pl.ds(half, half)], w_sem.at[1]),
        pltpu.make_async_copy(wd_hbm.at[0], wd_ref, w_sem.at[2]),
    ]
    loads = [
        pltpu.make_async_copy(up_hbm.at[0], x_ref.at[0], w_sem.at[3]),
        pltpu.make_async_copy(router_hbm, router_ref, w_sem.at[4]),
        pltpu.make_async_copy(su_hbm.at[0], slots_ref.at[0], w_sem.at[5]),
        pltpu.make_async_copy(sd_hbm.at[0], slots_ref.at[1], w_sem.at[6]),
        pltpu.make_async_copy(dn_hbm.at[0], x_ref.at[1], w_sem.at[7]),
    ]
    for copy in loads:
        copy.start()

    for copy in loads[:4]:
        copy.wait()
    for copy in weights:
        copy.start()
    first(0)
    for st in (0, 1):
        for p in (0, 1):
            mys_ref[p, st] = jnp.zeros(mys_ref.shape[2:], jnp.int32)
            mys_ref[p, st, 0:1, 0:tokens] = slots_ref[st, p]

        @pl.when(jnp.logical_not(has_next[st]))
        def _(st=st):
            nbs_ref[st] = jnp.zeros(nbs_ref.shape[1:], jnp.int32)

        @pl.when(jnp.logical_not(has_prev[st]))
        def _(st=st):
            prs_ref[st] = jnp.zeros(prs_ref.shape[1:], jnp.int32)
            dr_ref[st] = jnp.zeros(dr_ref.shape[1:], BF16)
            g_ref[1, st, 4 + x] = jnp.zeros(g_ref.shape[3:], BF16)
            xr_ref[st] = jnp.zeros(xr_ref.shape[1:], BF16)

    neighbours = 4 + 2 * (s > 0).astype(jnp.int32) + 2 * (s < sections - 1).astype(jnp.int32)
    pl.semaphore_wait(barrier, neighbours)

    def begin(st):
        if st == 1:
            loads[4].wait()
            first(1)
        for c in range(n):
            agz(0, st, c).start()

    def slots():
        for st in (0, 1):
            @pl.when(has_prev[st])
            def _(st=st):
                nslots(st).start()

            @pl.when(has_next[st])
            def _(st=st):
                oslots(st).start()

    def slots_sent():
        for st in (0, 1):
            pl.when(has_prev[st])(lambda st=st: nslots(st).wait_send())
            pl.when(has_next[st])(lambda st=st: oslots(st).wait_send())

    def weights_here():
        for w in weights:
            w.wait()

    def compute(p, st):
        gathered(p, st)
        hidden = gate_up(p, st)
        tails = []
        for c in range(n):
            down(p, st, hidden, tails, c)

    def send_rows(p, st):
        for c in (0, 1):
            rsa(p, st, c).start()
            rsd(p, st, c).start()

    def pass_rows(p, st):
        for c in (0, 1):
            rsa(p, st, c).wait_recv()
            total = p_ref[p, st, peer(way(c)), :, pieces[c]].astype(F32)
            total = total + ra_ref[p, st, :, pieces[c]].astype(F32)
            sb_ref[p, st, :, pieces[c]] = total.astype(BF16)
            rsb(p, st, c).start()

    steps = dict(
        begin=begin, send_own=send_own, slots=slots, slots_sent=slots_sent, weights=weights_here,
        relay=relay, own=arrive_own, compute=compute, send_rows=send_rows, pass_rows=pass_rows, relay_own=relay_own, reduce=reduce_other,
        finish_first=finish_first, send_shift=send_shift,
        finish_second=finish_second, sent_gather=sent_gather, sent_reduce=sent_reduce,
    )
    for name, *args in ORDER:
        steps[name](*args)
    for st in (0, 1):
        result(st).wait()


def shards(up_in, down_in, router, w_gate, w_up, w_down, slots_up, slots_down, *, sections):
    _, tokens, width = up_in.shape
    groups = width // G
    packed = width + G
    ends = [(groups + 1) * i // CHUNKS for i in range(CHUNKS + 1)]
    chunks = list(zip(ends[:-1], ends[1:]))
    n = len(chunks)
    ffd = w_gate.shape[2]
    hbm = pl.BlockSpec(memory_space=pl.ANY)
    dma = pltpu.SemaphoreType.DMA
    out = jax.ShapeDtypeStruct(up_in.shape, BF16)
    return pl.pallas_call(
        functools.partial(kernel_entry, chunks=chunks, sections=sections),
        name="relay_layers",
        out_shape=(out, out),
        in_specs=[hbm] * 8,
        out_specs=(hbm, hbm),
        scratch_shapes=[
            pltpu.VMEM((2, tokens, width), BF16),
            pltpu.VMEM((1, width), F32),
            pltpu.VMEM((2, 2, 1, tokens), jnp.int32),
            pltpu.VMEM((2, 2, 8, MAIN, packed), BF16),
            pltpu.VMEM((2, 2, 8, MAIN, packed), BF16),
            pltpu.VMEM((2, 2, MAIN, packed), BF16),
            pltpu.VMEM((2, 2, MAIN, packed), BF16),
            pltpu.VMEM((2, 2, MAIN, packed), BF16),
            pltpu.VMEM((2, 2, MAIN, packed), BF16),
            pltpu.VMEM((2, 2, 3, MAIN, packed), BF16),
            pltpu.VMEM((2, KEPT, width), BF16),
            pltpu.VMEM((2, KEPT, width), BF16),
            pltpu.VMEM((2, 2, MAIN, packed), BF16),
            pltpu.VMEM((2, 2, MAIN, packed), BF16),
            pltpu.VMEM((2, MAIN, packed), BF16),
            pltpu.VMEM((2, tokens, width), BF16),
            pltpu.VMEM((2, tokens, width), BF16),
            pltpu.VMEM((2, MAIN, packed), BF16),
            pltpu.VMEM((2, MAIN, packed), BF16),
            pltpu.VMEM((2, 2, tokens, 128), F32),
            pltpu.VMEM((2, 2, 8, 128), jnp.int32),
            pltpu.VMEM((2, 8, 128), jnp.int32),
            pltpu.VMEM((2, 8, 128), jnp.int32),
            pltpu.VMEM((width, 2 * ffd), BF16),
            pltpu.VMEM((ffd, width), BF16),
            dma((10,)),
            dma((2, 2, n)), dma((2, 2, n)),
            dma((2, 2, 3, n)), dma((2, 2, 3, n)),
            dma((2, 2, 2, 2)), dma((2, 2, 2, 2)),
            dma((2, 2, 2)), dma((2, 2, 2)),
            dma((2,)), dma((2,)),
            dma((2, 2, 3, n)), dma((2, 2, 3, n)),
            dma((2, 2, 2)), dma((2, 2, 2)),
            dma((2, 2, 2)), dma((2, 2, 2)),
            dma((2, 2, 2)), dma((2, 2, 2)),
            dma((2, 2, n)), dma((2, 2, n)),
            dma((2,)), dma((2,)),
            dma((2,)), dma((2,)),
            dma((2,)), dma((2,)),
        ],
        compiler_params=pltpu.CompilerParams(
            collective_id=0, has_side_effects=True, vmem_limit_bytes=VMEM_LIMIT
        ),
    )(up_in, down_in, router, slots_up, slots_down, w_gate, w_up, w_down)


def kernel_entry(*refs, chunks, sections):
    kernel(*refs[:35], chunks, sections, *refs[35:])


def solution(mesh):
    in_specs = (
        P("section", "expert", None),
        P("section", "expert", None),
        P("section", None),
        P("section", None, "expert"),
        P("section", None, "expert"),
        P("section", "expert", None),
        P("section", None, "expert", None),
        P("section", None, "expert", None),
    )
    out_specs = (P("section", "expert", None), P("section", "expert", None))
    body = functools.partial(shards, sections=mesh.shape["section"])
    return jax.shard_map(body, mesh=mesh, in_specs=in_specs, out_specs=out_specs, check_vma=False)
```
